32 devices in a mesh: tensor: 2 (over x), wide: 16 (over z, y, core).
Axes of the slice: x: 2, y: 2, z: 4, core: 2. Of those that a mesh axis runs over, the one named last changes fastest.
Arguments:
- tokens: bfloat16 [128, 3072], P('wide', 'tensor'), may hold values from -6 to 6
- cotangent: bfloat16 [128, 3072], P('wide', 'tensor'), may hold values from -1.5 to 1.5
- gates: bfloat16 [128, 2], P('wide'), may hold values from 0.19921875 to 1
- experts: int32 [128, 2], P('wide'), may hold values from 0 to 7, all different within a row; in each aligned block of 8 rows (0 to 7, 8 to 15, ...) at most 4 rows name the same one
- w_gate: bfloat16 [16, 3072, 4096], P('wide', None, 'tensor'), may hold values from -0.109375 to 0.109375
- w_up: bfloat16 [16, 3072, 4096], P('wide', None, 'tensor'), may hold values from -0.109375 to 0.109375
- w_down: bfloat16 [16, 4096, 3072], P('wide', 'tensor'), may hold values from -0.0625 to 0.0625
Outputs:
- input_grad: bfloat16 [128, 3072], P('wide', 'tensor')
- routing_grad: float32 [128, 2], P('wide')
- gate_proj_grad: bfloat16 [16, 3072, 4096], P('wide', None, 'tensor')
- up_proj_grad: bfloat16 [16, 3072, 4096], P('wide', None, 'tensor')
- down_proj_grad: bfloat16 [16, 4096, 3072], P('wide', 'tensor')
The draws below stay inside these ranges and needn't reach their ends.
Inputs may be any that keep to these rules, and one draw needn't show every extreme that they name: Each token names 2 different experts. Among the 8 tokens of one index of wide (aligned blocks of rows) no expert is named more than 4 times, and in every draw some expert is named exactly 4 times by some block.
All inputs are finite; a program needn't handle non-finite values.
Results may differ from the reference program's by a relative error of at most 0.02.
Values may be sent and summed in bfloat16 or wider, within the bound.
No kernel may reach another device: no remote copies, remote signals or barrier semaphores. Data moves between devices by JAX's collectives and lax.ppermute only.
A program may use at most 128 MiB of HBM per device.

```python
import math
import jax
import jax.numpy as jnp
import numpy as np

D = 3072
FF = 8192
E = 8
TOP = 2
TOK_DEV = 8
CAP = 4
FFR = 4096
SLABS = 16
TOKENS = 128
N_WIDE = 16


def levels(own_key, shape, pieces, low, high):
    loudness, own = 1.0, jax.random.fold_in(own_key, 6)
    for dim, shards_of in pieces:
        heights = jnp.exp(jax.random.uniform(jax.random.fold_in(own, dim), (shards_of,), jnp.float32, low / len(pieces), high / len(pieces)))
        loudness = loudness * jnp.repeat(heights, shape[dim] // shards_of).reshape([-1 if axis == dim else 1 for axis in range(len(shape))])
    return loudness


def shared_out(stream_key, own, number, rows, count, top, limit, skew):
    ranking = jax.random.permutation(stream_key, count)
    crowded, usual = shares(count, rows * top, limit, skew, True), shares(count, rows * top, limit, skew, False)
    places = jnp.arange(count)

    def named(sizes, offset_by):
        used = int((sizes > 0).sum())
        fixed = max(1, used // 4)
        passed = fixed + (places - fixed + offset_by * (used - fixed)) % max(1, count - fixed)
        return jnp.zeros((count,), jnp.int32).at[ranking[jnp.where(places < fixed, places, passed)]].set(jnp.asarray(sizes, jnp.int32))

    sizes = jnp.where(number % 4 == 0, named(crowded, number // 4), named(usual, number - number // 4 - 1))
    mixed = jax.random.permutation(jax.random.fold_in(own, 3), count)
    donor, taker = mixed[0:count // 2 * 2:2], mixed[1:count // 2 * 2:2]
    room = jnp.minimum(sizes[donor] - 1, limit - sizes[taker]) // 2
    room = jnp.where((donor == ranking[0]) | (taker == ranking[0]) | (sizes[taker] == 0), 0, jnp.maximum(room, 0))
    passed = jax.random.randint(jax.random.fold_in(own, 4), (count // 2,), 0, 1 << 20) % (room + 1)
    sizes = sizes.at[donor].add(-passed).at[taker].add(passed)
    labels = jnp.searchsorted(jnp.cumsum(sizes), jnp.arange(rows * top), side="right").astype(jnp.int32)
    grid = labels.reshape(top, rows).T
    grid = grid[jax.random.permutation(jax.random.fold_in(own, 1), rows)]
    offset_by = jax.random.randint(jax.random.fold_in(own, 2), (rows, 1), 0, top)
    return jnp.take_along_axis(grid, (jnp.arange(top)[None, :] + offset_by) % top, axis=1)


def shares(amount, total, most, lean, full):
    weights = [(1 << 20) // math.isqrt(standing ** lean) + 1 for standing in range(1, amount + 1)]
    largest = most if full else min(most, max(-(-total // amount), total * weights[0] // sum(weights)))
    least = 1 if total - largest >= amount - 1 else 0
    given, rest = [largest] + [least] * (amount - 1), total - largest - least * (amount - 1)
    while rest > 0:
        free = [i for i in range(1, amount) if given[i] < largest] or [i for i in range(1, amount) if given[i] < most]
        whole, budget = sum([weights[i] for i in free]), rest
        for i in free:
            extra = min(most - given[i], max(1, budget * weights[i] // whole), rest)
            given[i] = given[i] + extra
            rest = rest - extra
    return np.array(given)


def gaussian(stream_key, shape, spread, limit, shards=(), kind=jnp.bfloat16):
    gain = levels(stream_key, shape, shards, -0.22, 0.18) if shards else 1.0
    drawn = jax.random.normal(stream_key, shape, jnp.float32) * spread * gain
    return jnp.minimum(jnp.maximum(drawn, -limit), limit).astype(kind)


def setup_inputs(seed: int = 0) -> dict:
    streams_of = jax.random.split(jax.random.key(seed), 8)
    tokens = gaussian(streams_of[0], (TOKENS, D), 1.0, 6.0, ((0, 16), (1, 2)))
    cotangent = gaussian(streams_of[1], (TOKENS, D), 0.25, 1.5, ((0, 16), (1, 2)))
    gates = jnp.clip(0.19921875 + 0.80078125 * jax.random.uniform(streams_of[2], (TOKENS, TOP), jnp.float32) ** levels(streams_of[2], (TOKENS, TOP), ((0, 16),), -0.2, 0.2), 0.19921875, 1.0).astype(jnp.bfloat16)
    experts_keys = jax.random.split(jax.random.fold_in(streams_of[3], 1), TOKENS // TOK_DEV)
    experts_turns = jax.random.permutation(jax.random.fold_in(streams_of[3], 3), TOKENS // TOK_DEV)
    experts = jax.vmap(lambda own, number: shared_out(jax.random.fold_in(streams_of[3], 2), own, number, TOK_DEV, E, TOP, CAP, 2))(experts_keys, experts_turns).reshape((TOKENS, TOP))
    w_gate = gaussian(streams_of[4], (SLABS, D, FFR), D ** -0.5, 0.109375, ((0, 16), (2, 2)))
    w_up = gaussian(streams_of[5], (SLABS, D, FFR), D ** -0.5, 0.109375, ((0, 16), (2, 2)))
    w_down = gaussian(streams_of[6], (SLABS, FFR, D), FF ** -0.5, 0.0625, ((0, 16), (1, 2)))
    return {"tokens": tokens, "cotangent": cotangent, "gates": gates, "experts": experts, "w_gate": w_gate, "w_up": w_up, "w_down": w_down}


def reference(tokens, cotangent, gates, experts, w_gate, w_up, w_down):
    slot_rows = N_WIDE * CAP
    replicas = N_WIDE // E
    hidden_all = FFR * replicas
    gate_full = w_gate.reshape(E, replicas, D, FFR).transpose(0, 2, 1, 3).reshape(E, D, hidden_all)
    up_full = w_up.reshape(E, replicas, D, FFR).transpose(0, 2, 1, 3).reshape(E, D, hidden_all)
    down_full = w_down.reshape(E, hidden_all, D)
    input_grad = jnp.zeros((TOKENS, D), jnp.float32)
    routing_grad = jnp.zeros((TOKENS, TOP), jnp.float32)
    gate_grads = []
    up_grads = []
    down_grads = []
    for expert in range(E):
        chosen = experts == expert
        picked = jnp.any(chosen, axis=1)
        weight = jnp.sum(jnp.where(chosen, gates.astype(jnp.float32), 0.0), axis=1)
        where_rows = jnp.nonzero(picked, size=slot_rows, fill_value=0)[0]
        live_rows = (jnp.arange(slot_rows) < jnp.sum(picked.astype(jnp.int32))).astype(jnp.float32)
        inputs = tokens[where_rows]
        upstream = cotangent[where_rows]
        slot_scale = weight[where_rows] * live_rows
        pre_gate = jnp.dot(inputs, gate_full[expert], preferred_element_type=jnp.float32)
        pre_up = jnp.dot(inputs, up_full[expert], preferred_element_type=jnp.float32)
        sigmoid_gate = jax.nn.sigmoid(pre_gate)
        active = pre_gate * sigmoid_gate
        hidden = active * pre_up
        weighted = (slot_scale[:, None] * hidden).astype(jnp.bfloat16)
        through = jnp.dot(upstream, down_full[expert].T, preferred_element_type=jnp.float32)
        gate_terms = jnp.sum(through * hidden, axis=1) * live_rows
        hidden_grad = slot_scale[:, None] * through
        grad_pre_gate = (hidden_grad * pre_up * sigmoid_gate * (1.0 + pre_gate * (1.0 - sigmoid_gate))).astype(jnp.bfloat16)
        grad_pre_up = (hidden_grad * active).astype(jnp.bfloat16)
        gate_grads.append(jnp.dot(inputs.T, grad_pre_gate, preferred_element_type=jnp.float32).astype(jnp.bfloat16))
        up_grads.append(jnp.dot(inputs.T, grad_pre_up, preferred_element_type=jnp.float32).astype(jnp.bfloat16))
        down_grads.append(jnp.dot(weighted.T, upstream, preferred_element_type=jnp.float32).astype(jnp.bfloat16))
        returned = jnp.dot(grad_pre_gate, gate_full[expert].T, preferred_element_type=jnp.float32)
        returned = returned + jnp.dot(grad_pre_up, up_full[expert].T, preferred_element_type=jnp.float32)
        input_grad = input_grad.at[where_rows].add(returned * live_rows[:, None])
        routing_grad = routing_grad.at[where_rows].add(jnp.where(chosen[where_rows], gate_terms[:, None], 0.0))
    gate_stack = jnp.stack(gate_grads).reshape(E, D, replicas, FFR).transpose(0, 2, 1, 3).reshape(E * replicas, D, FFR)
    up_stack = jnp.stack(up_grads).reshape(E, D, replicas, FFR).transpose(0, 2, 1, 3).reshape(E * replicas, D, FFR)
    down_stack = jnp.stack(down_grads).reshape(E * replicas, FFR, D)
    return (input_grad.astype(jnp.bfloat16), routing_grad, gate_stack, up_stack, down_stack)
```

```python
import functools

import jax
import jax.numpy as jnp
from jax import lax
from jax.experimental import pallas as pl
from jax.experimental.pallas import tpu as pltpu
from jax.sharding import PartitionSpec as P

E = 8
CAP = 4
LANES = 128
BF = jnp.bfloat16
F32 = jnp.float32
VMEM = pl.BlockSpec(memory_space=pltpu.VMEM)
SMEM = pl.BlockSpec(memory_space=pltpu.SMEM)
ANY = pl.BlockSpec(memory_space=pl.ANY)


def dot(left, right, left_dim, right_dim):
    return lax.dot_general(
        left, right, (((left_dim,), (right_dim,)), ((), ())), preferred_element_type=F32
    )


def params(mib):
    return pltpu.CompilerParams(vmem_limit_bytes=mib << 20)


def cost(flops, moved):
    return pl.CostEstimate(flops=flops, bytes_accessed=moved, transcendentals=0)


def column(row):
    n = row.shape[1]
    sub = lax.broadcasted_iota(jnp.int32, (n, n), 0)
    lane = lax.broadcasted_iota(jnp.int32, (n, n), 1)
    return jnp.sum(jnp.where(sub == lane, jnp.broadcast_to(row, (n, n)), 0.0), axis=1, keepdims=True)


def routing(experts_ref, lane_expert):
    ids = experts_ref[...].astype(F32)
    first, second = column(ids[0:1, :]), column(ids[1:2, :])
    hit_first = lane_expert == first
    hit_second = lane_expert == second
    picked = jnp.where(hit_first | hit_second, 1.0, 0.0)
    sub = lax.broadcasted_iota(jnp.int32, picked.shape, 0)
    before = jnp.zeros_like(picked)
    for row in range(picked.shape[0] - 1):
        before = before + jnp.where(sub > row, picked[row : row + 1, :], 0.0)
    return hit_first, hit_second, picked, before


def pack_kernel(tokens_ref, cotangent_ref, gates_ref, experts_ref, out_ref):
    width = tokens_ref.shape[1]
    rows = tokens_ref.shape[0]
    lane = lax.broadcasted_iota(jnp.int32, (rows, LANES), 1)
    lane_expert = (lane % E).astype(F32)
    hit_first, hit_second, picked, before = routing(experts_ref, lane_expert)
    gates = gates_ref[...].astype(F32)
    gate = jnp.where(hit_first, column(gates[0:1, :]), 0.0) + jnp.where(
        hit_second, column(gates[1:2, :]), 0.0
    )
    place = jnp.where(picked > 0.5, before, -1.0)
    info = jnp.where(lane < E, place, jnp.where(lane < 2 * E, gate, 0.0))
    out_ref[:, :width] = tokens_ref[...]
    out_ref[:, width : 2 * width] = cotangent_ref[...]
    out_ref[:, 2 * width :] = info.astype(BF)


def stage_kernel(parts, position_ref, after_ref, source_ref, out_ref, token_ref, sems):
    width = out_ref.shape[0] // len(parts)
    copies = []
    for i, mask in enumerate(parts):
        start = pl.multiple_of((position_ref[0] ^ mask) * width, width)
        copies.append(
            pltpu.make_async_copy(
                source_ref.at[pl.ds(start, width)], out_ref.at[pl.ds(i * width, width)], sems.at[i]
            )
        )
    for copy in copies:
        copy.start()
    token_ref[...] = jnp.zeros_like(token_ref)
    for copy in copies:
        copy.wait()


def stage(position, weight, parts, width, after):
    rows, columns = width * len(parts), weight.shape[1]
    return pl.pallas_call(
        functools.partial(stage_kernel, parts),
        out_shape=[pltpu.VMEM((rows, columns), BF), pltpu.VMEM((8, LANES), F32)],
        in_specs=[SMEM, ANY, ANY],
        out_specs=[ANY, VMEM],
        scratch_shapes=[pltpu.SemaphoreType.DMA((len(parts),))],
        compiler_params=params(4),
        cost_estimate=cost(0, 4 * rows * columns),
        name="stage",
    )(position, after, pltpu.with_memory_space_constraint(weight, pltpu.HBM))


def join_kernel(own_ref, got_ref, *refs):
    out_ref = refs[-1]
    rows = own_ref.shape[0]
    out_ref[:rows, :] = own_ref[...]
    out_ref[rows:, :] = got_ref[...]


def select_kernel(expert_ref, own_ref, got_ref, *refs):
    out_ref = refs[-1]
    expert = expert_ref[0]
    tok_rows, full = own_ref.shape
    slots = out_ref.shape[0]
    blocks = slots // CAP // 2
    per_block = tok_rows // blocks
    total = jnp.zeros((slots, full), F32)
    for side, ref in enumerate((own_ref, got_ref)):
        info = ref[:, full - LANES :].astype(F32)
        lane = lax.broadcasted_iota(jnp.int32, info.shape, 1)
        place = jnp.sum(jnp.where(lane == expert, info, 0.0), axis=1, keepdims=True)
        row = lax.broadcasted_iota(jnp.int32, (tok_rows, slots), 0)
        col = lax.broadcasted_iota(jnp.int32, (tok_rows, slots), 1)
        take = (row // per_block + side * blocks == col // CAP) & (place == (col % CAP).astype(F32))
        total = total + dot(jnp.where(take, 1.0, 0.0).astype(BF), ref[...], 0, 0)
    out_ref[...] = total.astype(BF)


def stacked(refs, start, size):
    return jnp.concatenate([ref[:, start : start + size] for ref in refs], axis=0)


def down_copies(tiles, tile, places, w_down, buffer, sems):
    return [
        [
            pltpu.make_async_copy(
                w_down.at[pl.ds(i * tile, tile), place], buffer.at[m, pl.ds(i * tile, tile)], sems.at[m, i]
            )
            for m, place in enumerate(places)
        ]
        for i in range(tiles)
    ]


def first_kernel(replicas, position_ref, *refs):
    parts = refs[:replicas]
    w_gate, w_up, w_down, gate_out, up_out, through_out, buffer, sems = refs[replicas:]
    width = (parts[0].shape[1] - LANES) // 2
    here = pl.ds(pl.multiple_of(position_ref[0] * width, width), width)
    hidden = w_gate.shape[1]
    tiles = sems.shape[1]
    tile = hidden // tiles
    copies = down_copies(tiles, tile, [here], w_down, buffer, sems)
    for row in copies:
        row[0].start()
    inputs = stacked(parts, 0, width)
    upstream = stacked(parts, width, width)
    for i in range(tiles):
        units = slice(i * tile, (i + 1) * tile)
        gate_out[:, units] = dot(inputs, w_gate[:, units], 1, 0)
        up_out[:, units] = dot(inputs, w_up[:, units], 1, 0)
        copies[i][0].wait()
        through_out[:, units] = dot(upstream, buffer[0, units, :], 1, 1)


def second_kernel(replicas, others, position_ref, *refs):
    own = refs[:replicas]
    parts = [refs[replicas * (m + 1) : replicas * (m + 2)] for m in range(others)]
    rest = refs[replicas * (others + 1) :]
    w_gate, w_up, w_down, gate_in, up_in, through_in = rest[:6]
    weighted_ref, grad_gate_ref, grad_up_ref, inputs_ref, upstream_ref, routing_ref = rest[6:12]
    buffer, sems = rest[12:]
    full = own[0].shape[1]
    width = (full - LANES) // 2
    position, expert = position_ref[0], position_ref[1]
    places = [pl.ds(pl.multiple_of((position ^ m) * width, width), width) for m in range(others + 1)]
    hidden = w_gate.shape[1]
    tiles = sems.shape[1]
    tile = hidden // tiles
    copies = down_copies(tiles, tile, places[1:], w_down, buffer, sems)
    for row in copies:
        for copy in row:
            copy.start()
    info = stacked(own, full - LANES, LANES).astype(F32)
    lane = lax.broadcasted_iota(jnp.int32, info.shape, 1)
    scale = jnp.sum(jnp.where(lane == expert + E, info, 0.0), axis=1, keepdims=True)
    for m, blocks in enumerate([own] + parts):
        inputs_ref[:, places[m]] = stacked(blocks, 0, width)
        upstream_ref[:, places[m]] = stacked(blocks, width, width)
    x = jnp.concatenate([stacked(part, 0, width) for part in parts], axis=1)
    score = jnp.zeros_like(routing_ref)
    for i in range(tiles):
        units = slice(i * tile, (i + 1) * tile)
        pre_gate = gate_in[:, units] + dot(x, w_gate[:, units], 1, 0)
        pre_up = up_in[:, units] + dot(x, w_up[:, units], 1, 0)
        through = through_in[:, units]
        for m in range(others):
            copies[i][m].wait()
            through = through + dot(stacked(parts[m], width, width), buffer[m, units, :], 1, 1)
        sig = jax.nn.sigmoid(pre_gate)
        act = pre_gate * sig
        product = act * pre_up
        weighted_ref[:, units] = (scale * product).astype(BF)
        score = score + jnp.sum(through * product, axis=1, keepdims=True)
        scaled = scale * through
        grad_gate_ref[:, units] = (scaled * pre_up * sig * (1.0 + pre_gate * (1.0 - sig))).astype(BF)
        grad_up_ref[:, units] = (scaled * act).astype(BF)
    routing_ref[...] = score


def halves(value, shape):
    high = value.astype(BF).astype(F32)
    lane = lax.broadcasted_iota(jnp.int32, shape, 1)
    return jnp.where(lane == 0, high, jnp.where(lane == 1, value - high, 0.0)).astype(BF)


def joined(lanes):
    lane = lax.broadcasted_iota(jnp.int32, lanes.shape, 1)
    return jnp.sum(jnp.where(lane < 2, lanes.astype(F32), 0.0), axis=1, keepdims=True)


def back_kernel(grad_gate, grad_up, w_gate, w_up, routing_ref, out_ref):
    width = w_gate.shape[0]
    part = dot(w_gate[...], grad_gate[...], 1, 1) + dot(w_up[...], grad_up[...], 1, 1)
    out_ref[:, :width] = part.astype(out_ref.dtype).T
    if out_ref.shape[1] > width:
        out_ref[:, width:] = halves(routing_ref[...], (out_ref.shape[0], LANES))


def back_other_kernel(others, *refs):
    grad_gate, grad_up, w_gate, w_up, routing_ref = refs[:5]
    outs = refs[5:]
    width = w_gate.shape[0] // others
    for m, out_ref in enumerate(outs):
        rows = pl.ds(m * width, width)
        back_kernel(grad_gate, grad_up, w_gate.at[rows], w_up.at[rows], routing_ref, out_ref)


def merge_kernel(replicas, offsets, position_ref, own_ref, routing_ref, *refs):
    parts, out_ref = refs[:-1], refs[-1]
    slots, width = own_ref.shape
    half = out_ref.shape[1]
    total = own_ref[...]
    score = routing_ref[...]
    for part in parts:
        total = total + part[:, :width].astype(F32)
        score = score + joined(part[:, width:])
    rows = jnp.concatenate(
        [total.astype(BF), halves(score, (slots, 2 * half - width))], axis=1
    )
    place = position_ref[2]
    out_row = lax.broadcasted_iota(jnp.int32, (2 * slots, slots), 0)
    slot = lax.broadcasted_iota(jnp.int32, (2 * slots, slots), 1)
    blocks = len(offsets)
    origin = jnp.zeros_like(slot)
    for r in range(replicas):
        for j, offset in enumerate(offsets):
            origin = jnp.where(slot // CAP == r * blocks + j, offset ^ r, origin)
    origin = origin ^ place
    lands = (out_row // (2 * CAP) == origin) & (out_row % CAP == slot % CAP)
    low = lands & (out_row % (2 * CAP) < CAP)
    high = lands & (out_row % (2 * CAP) >= CAP)
    out = dot(jnp.where(low, 1.0, 0.0).astype(BF), rows[:, :half], 1, 0)
    out = out + dot(jnp.where(high, 1.0, 0.0).astype(BF), rows[:, half:], 1, 0)
    out_ref[...] = out.astype(BF)


def finish_kernel(replicas, back_ref, experts_ref, grad_ref, routing_ref):
    rows, half = back_ref.shape
    tok, width = grad_ref.shape
    lane = lax.broadcasted_iota(jnp.int32, (tok, rows), 1)
    lane_expert = ((lane // (2 * CAP)) // replicas).astype(F32)
    hit_first, hit_second, _, before = routing(experts_ref, lane_expert)
    here = before == (lane % CAP).astype(F32)
    low = lane % (2 * CAP) < CAP
    any_hit = (hit_first | hit_second) & here

    def gather(mask, part):
        return dot(jnp.where(mask, 1.0, 0.0).astype(BF), part, 1, 0)

    grad_ref[:, :half] = gather(any_hit & low, back_ref[...]).astype(BF)
    tail = back_ref[:, : width - half]
    grad_ref[:, half:] = gather(any_hit & ~low, tail).astype(BF)
    score = back_ref[:, width - half : width - half + LANES]
    outs = [joined32(gather(hit & here & ~low, score)) for hit in (hit_first, hit_second)]
    sub = lax.broadcasted_iota(jnp.int32, (tok, tok), 0)
    diagonal = lax.broadcasted_iota(jnp.int32, (tok, tok), 1)
    for k, out in enumerate(outs):
        spread = jnp.where(sub == diagonal, jnp.broadcast_to(out, (tok, tok)), 0.0)
        routing_ref[k : k + 1, :] = jnp.sum(spread, axis=0, keepdims=True)


def joined32(lanes):
    lane = lax.broadcasted_iota(jnp.int32, lanes.shape, 1)
    return jnp.sum(jnp.where(lane < 2, lanes, 0.0), axis=1, keepdims=True)


def outer_kernel(tile, depth, count, *refs):
    lefts, rights, outs = refs[:count], refs[count : 2 * count], refs[2 * count : 3 * count]
    buffer, sems = refs[3 * count :]
    steps = []
    for left, right, out in zip(lefts, rights, outs):
        rows, columns = out.shape
        steps += [(left, right, out, start) for start in range(0, rows, tile)]
    copies = []
    for i, (left, right, out, start) in enumerate(steps):
        slot = i % depth
        if i >= depth:
            copies[i - depth].wait()
        columns = out.shape[1]
        place = buffer.at[slot, :, pl.ds(0, columns)]
        place[...] = dot(left[:, start : start + tile], right[...], 0, 0).astype(BF)
        copies.append(pltpu.make_async_copy(place, out.at[pl.ds(start, tile)], sems.at[slot]))
        copies[i].start()
    for copy in copies[max(0, len(copies) - depth) :]:
        copy.wait()


def outer(pairs, name):
    shapes = [(left.shape[1], right.shape[1]) for left, right in pairs]
    tile = min([512] + [rows for rows, _ in shapes])
    tile = next(size for size in (tile, 384, 256, 128) if all(rows % size == 0 for rows, _ in shapes))
    slots = pairs[0][0].shape[0]
    depth = 4
    widest = max(columns for _, columns in shapes)
    size = sum(rows * columns for rows, columns in shapes)
    return pl.pallas_call(
        functools.partial(outer_kernel, tile, depth, len(pairs)),
        out_shape=[jax.ShapeDtypeStruct(shape, BF) for shape in shapes],
        in_specs=[VMEM] * (2 * len(pairs)),
        out_specs=[ANY] * len(pairs),
        scratch_shapes=[pltpu.VMEM((depth, tile, widest), BF), pltpu.SemaphoreType.DMA((depth,))],
        compiler_params=params(20),
        cost_estimate=cost(8 * slots * size, 2 * size),
        name=name,
    )(*[left for left, _ in pairs], *[right for _, right in pairs])


def shards(n_wide, n_tensor, tokens, cotangent, gates, experts, w_gate, w_up, w_down):
    axes = ("tensor", "wide")
    replicas = n_wide // E
    wide, tensor = lax.axis_index("wide"), lax.axis_index("tensor")
    tok, width = tokens.shape
    hidden = w_gate.shape[2]
    full = 2 * width + LANES
    slots = n_wide * CAP
    position = jnp.stack([tensor, wide // replicas, wide]).astype(jnp.int32)
    expert = (wide // replicas).astype(jnp.int32)[None]

    def swap(value, wide_mask, tensor_mask):
        pairs = [
            (t * n_wide + w, (t ^ tensor_mask) * n_wide + (w ^ wide_mask))
            for t in range(n_tensor)
            for w in range(n_wide)
        ]
        return lax.ppermute(value, axes, pairs)

    def shape(rows, columns, dtype=BF):
        return jax.ShapeDtypeStruct((rows, columns), dtype)

    experts_t = experts.T
    own = (0,)
    rest = tuple(range(1, n_tensor))
    gathered = pl.pallas_call(
        pack_kernel,
        out_shape=pltpu.VMEM((tok, full), BF),
        in_specs=[VMEM] * 4,
        out_specs=VMEM,
        compiler_params=params(2),
        name="pack",
    )(tokens, cotangent, gates.T, experts_t)

    plan = [(w_gate[0], own), (w_up[0], own), (w_gate[0], rest), (w_up[0], rest)]
    staged = []
    offsets = [0]
    mask = n_wide // 2
    while mask >= replicas:
        last = mask == replicas
        got = swap(gathered, mask, 0)
        tokens_done = []
        for weight, which in plan[len(staged) : len(plan) if last else len(staged) + 1]:
            kept_weight, token = stage(position, weight, which, width, gathered)
            staged.append(kept_weight)
            tokens_done.append(token)
        if not last:
            gathered = pl.pallas_call(
                join_kernel,
                out_shape=pltpu.VMEM((2 * gathered.shape[0], full), BF),
                in_specs=[VMEM] * 2 + [ANY] * len(tokens_done),
                out_specs=VMEM,
                compiler_params=params(4),
        name="join",
            )(gathered, got, *tokens_done)
        offsets = offsets + [offset ^ mask for offset in offsets]
        mask //= 2

    chosen = pl.pallas_call(
        select_kernel,
        out_shape=pltpu.VMEM((slots // replicas, full), BF),
        in_specs=[SMEM, VMEM, VMEM] + [ANY] * len(tokens_done),
        out_specs=VMEM,
        compiler_params=params(6),
        name="select",
    )(expert, gathered, got, *tokens_done)
    wg_own, wu_own, wg_rest, wu_rest = staged
    away = [swap(chosen, 0, m) for m in rest]
    near = [chosen] + [swap(chosen, r, 0) for r in range(1, replicas)]

    tiles = max(1, hidden // 512)
    others = n_tensor - 1
    down = pltpu.with_memory_space_constraint(w_down[0], pltpu.HBM)
    partial = pl.pallas_call(
        functools.partial(first_kernel, replicas),
        out_shape=[shape(slots, hidden, F32)] * 3,
        in_specs=[SMEM] + [VMEM] * (replicas + 2) + [ANY],
        out_specs=[VMEM] * 3,
        scratch_shapes=[pltpu.VMEM((1, hidden, width), BF), pltpu.SemaphoreType.DMA((1, tiles))],
        compiler_params=params(16),
        cost_estimate=cost(24 * slots * width * hidden, 6 * width * hidden),
        name="first",
    )(position, *near, wg_own, wu_own, down)

    parts = [[part] + [swap(part, r, 0) for r in range(1, replicas)] for part in away]
    weighted, grad_gate, grad_up, inputs, upstream, score = pl.pallas_call(
        functools.partial(second_kernel, replicas, others),
        out_shape=[shape(slots, hidden)] * 3
        + [shape(slots, width * n_tensor)] * 2
        + [shape(slots, 1, F32)],
        in_specs=[SMEM] + [VMEM] * (replicas * n_tensor + 2) + [ANY] + [VMEM] * 3,
        out_specs=[VMEM] * 6,
        scratch_shapes=[pltpu.VMEM((others, hidden, width), BF), pltpu.SemaphoreType.DMA((others, tiles))],
        compiler_params=params(16),
        cost_estimate=cost(24 * slots * width * hidden, 6 * width * hidden),
        name="second",
    )(position, *near, *sum(parts, []), wg_rest, wu_rest, down, *partial)

    sent = pl.pallas_call(
        functools.partial(back_other_kernel, others),
        out_shape=[shape(slots, width + LANES)] * others,
        in_specs=[VMEM] * 5,
        out_specs=[VMEM] * others,
        compiler_params=params(12),
        cost_estimate=cost(16 * slots * width * hidden, 4 * width * hidden),
        name="back_other",
    )(grad_gate, grad_up, wg_rest, wu_rest, score)
    returned = [swap(value, 0, m) for m, value in zip(rest, sent)]
    kept = pl.pallas_call(
        back_kernel,
        out_shape=shape(slots, width, F32),
        in_specs=[VMEM] * 5,
        out_specs=VMEM,
        compiler_params=params(12),
        cost_estimate=cost(16 * slots * width * hidden, 4 * width * hidden),
        name="back_own",
    )(grad_gate, grad_up, wg_own, wu_own, score)
    (gate_proj_grad,) = outer([(inputs, grad_gate)], "gate_grad")
    half = (width + 2 * LANES) // 2
    merged = pl.pallas_call(
        functools.partial(merge_kernel, replicas, offsets),
        out_shape=shape(2 * slots, half),
        in_specs=[SMEM] + [VMEM] * (2 + others),
        out_specs=VMEM,
        compiler_params=params(8),
        name="merge",
    )(position, kept, score, *returned)
    landed = lax.all_to_all(merged, "wide", split_axis=0, concat_axis=0, tiled=True)
    up_proj_grad, down_proj_grad = outer([(inputs, grad_up), (weighted, upstream)], "other_grads")
    input_grad, routing_grad = pl.pallas_call(
        functools.partial(finish_kernel, replicas),
        out_shape=[shape(tok, width), shape(2, tok, F32)],
        in_specs=[VMEM] * 2,
        out_specs=[VMEM] * 2,
        compiler_params=params(8),
        name="finish",
    )(landed, experts_t)
    return (
        input_grad,
        routing_grad.T,
        gate_proj_grad[None],
        up_proj_grad[None],
        down_proj_grad[None],
    )


def solution(mesh):
    return jax.shard_map(
        functools.partial(shards, mesh.shape["wide"], mesh.shape["tensor"]),
        mesh=mesh,
        in_specs=(
            P("wide", "tensor"),
            P("wide", "tensor"),
            P("wide", None),
            P("wide", None),
            P("wide", None, "tensor"),
            P("wide", None, "tensor"),
            P("wide", "tensor", None),
        ),
        out_specs=(
            P("wide", "tensor"),
            P("wide", None),
            P("wide", None, "tensor"),
            P("wide", None, "tensor"),
            P("wide", "tensor", None),
        ),
        check_vma=False,
    )
```

```python
import functools

import jax
import jax.numpy as jnp
from jax import lax
from jax.experimental import pallas as pl
from jax.experimental.pallas import tpu as pltpu
from jax.sharding import PartitionSpec as P

E = 8
CAP = 4
LANES = 128
BF = jnp.bfloat16
F32 = jnp.float32
VMEM = pl.BlockSpec(memory_space=pltpu.VMEM)
SMEM = pl.BlockSpec(memory_space=pltpu.SMEM)
ANY = pl.BlockSpec(memory_space=pl.ANY)


def dot(left, right, left_dim, right_dim):
    return lax.dot_general(
        left, right, (((left_dim,), (right_dim,)), ((), ())), preferred_element_type=F32
    )


def params(mib):
    return pltpu.CompilerParams(vmem_limit_bytes=mib << 20)


def cost(flops, moved):
    return pl.CostEstimate(flops=flops, bytes_accessed=moved, transcendentals=0)


def column(row):
    n = row.shape[1]
    sub = lax.broadcasted_iota(jnp.int32, (n, n), 0)
    lane = lax.broadcasted_iota(jnp.int32, (n, n), 1)
    return jnp.sum(jnp.where(sub == lane, jnp.broadcast_to(row, (n, n)), 0.0), axis=1, keepdims=True)


def routing(experts_ref, lane_expert):
    ids = experts_ref[...].astype(F32)
    first, second = column(ids[0:1, :]), column(ids[1:2, :])
    hit_first = lane_expert == first
    hit_second = lane_expert == second
    picked = jnp.where(hit_first | hit_second, 1.0, 0.0)
    sub = lax.broadcasted_iota(jnp.int32, picked.shape, 0)
    before = jnp.zeros_like(picked)
    for row in range(picked.shape[0] - 1):
        before = before + jnp.where(sub > row, picked[row : row + 1, :], 0.0)
    return hit_first, hit_second, picked, before


def pack_kernel(
    tokens_hbm, cotangent_hbm, gates_hbm, experts_hbm, out_ref, gates_ref, experts_ref, sems
):
    rows, width = tokens_hbm.shape
    copies = [
        pltpu.make_async_copy(source, target, sems.at[i])
        for i, (source, target) in enumerate(
            (
                (gates_hbm, gates_ref),
                (experts_hbm, experts_ref),
                (tokens_hbm, out_ref.at[:, pl.ds(0, width)]),
                (cotangent_hbm, out_ref.at[:, pl.ds(width, width)]),
            )
        )
    ]
    for copy in copies:
        copy.start()
    copies[0].wait()
    copies[1].wait()
    lane = lax.broadcasted_iota(jnp.int32, (rows, LANES), 1)
    lane_expert = (lane % E).astype(F32)
    hit_first, hit_second, picked, before = routing(experts_ref, lane_expert)
    gates = gates_ref[...].astype(F32)
    gate = jnp.where(hit_first, column(gates[0:1, :]), 0.0) + jnp.where(
        hit_second, column(gates[1:2, :]), 0.0
    )
    place = jnp.where(picked > 0.5, before, -1.0)
    info = jnp.where(lane < E, place, jnp.where(lane < 2 * E, gate, 0.0))
    out_ref[:, 2 * width :] = info.astype(BF)
    copies[2].wait()
    copies[3].wait()


def part_copies(position, by_row, masks, source, target, sems):
    copies = []
    for i, mask in enumerate(masks):
        if by_row:
            width = target.shape[0] // len(masks)
            place = pl.ds(pl.multiple_of((position ^ mask) * width, width), width)
            pair = (source.at[place], target.at[pl.ds(i * width, width)])
        else:
            width = target.shape[1]
            depth = target.shape[0] // len(masks)
            place = pl.ds(pl.multiple_of((position ^ mask) * width, width), width)
            pair = (source.at[:, place], target.at[pl.ds(i * depth, depth)])
        copies.append(pltpu.make_async_copy(*pair, sems.at[i]))
    return copies


def part_shape(weight, by_row, masks, width):
    if by_row:
        return pltpu.VMEM((width * len(masks), weight.shape[1]), BF)
    return pltpu.VMEM((weight.shape[0] * len(masks), width), BF)


def stage_kernel(jobs, position_ref, after_ref, *refs):
    count = len(jobs)
    sources, outs = refs[:count], refs[count : 2 * count]
    token_ref = refs[2 * count]
    copies = []
    for (by_row, masks), source, out, sems in zip(jobs, sources, outs, refs[2 * count + 1 :]):
        copies += part_copies(position_ref[0], by_row, masks, source, out, sems)
    for copy in copies:
        copy.start()
    token_ref[...] = jnp.zeros_like(token_ref)
    for copy in copies:
        copy.wait()


def stage(position, jobs, width, after):
    outs = [part_shape(*job, width) for job in jobs]
    size = sum(out.shape[0] * out.shape[1] for out in outs)
    *kept, token = pl.pallas_call(
        functools.partial(stage_kernel, [job[1:] for job in jobs]),
        out_shape=outs + [pltpu.VMEM((8, LANES), F32)],
        in_specs=[SMEM, ANY] + [ANY] * len(jobs),
        out_specs=[ANY] * len(jobs) + [VMEM],
        scratch_shapes=[pltpu.SemaphoreType.DMA((len(job[2]),)) for job in jobs],
        compiler_params=params(2),
        cost_estimate=cost(0, 4 * size),
        name="stage",
    )(position, after, *[pltpu.with_memory_space_constraint(job[0], pltpu.HBM) for job in jobs])
    return kept, token


def join_kernel(own_ref, got_ref, *refs):
    out_ref = refs[-1]
    rows = own_ref.shape[0]
    out_ref[:rows, :] = own_ref[...]
    out_ref[rows:, :] = got_ref[...]


def relay_kernel(value_ref, *refs):
    refs[-1][...] = value_ref[...]


def relay(value, after):
    return pl.pallas_call(
        relay_kernel,
        out_shape=pltpu.VMEM(value.shape, value.dtype),
        in_specs=[VMEM, ANY],
        out_specs=VMEM,
        compiler_params=params(2),
        name="relay",
    )(value, after)


def select_kernel(expert_ref, source_ref, *refs):
    out_ref = refs[-1]
    tok_rows, full = source_ref.shape
    slots = out_ref.shape[0]
    per_block = tok_rows // (slots // CAP)
    info = source_ref[:, full - LANES :].astype(F32)
    lane = lax.broadcasted_iota(jnp.int32, info.shape, 1)
    place = jnp.sum(jnp.where(lane == expert_ref[0], info, 0.0), axis=1, keepdims=True)
    row = lax.broadcasted_iota(jnp.int32, (tok_rows, slots), 0)
    col = lax.broadcasted_iota(jnp.int32, (tok_rows, slots), 1)
    take = (row // per_block == col // CAP) & (place == (col % CAP).astype(F32))
    out_ref[...] = dot(jnp.where(take, 1.0, 0.0).astype(BF), source_ref[...], 0, 0).astype(BF)


def select(expert, source, blocks, after):
    return pl.pallas_call(
        select_kernel,
        out_shape=pltpu.VMEM((blocks * CAP, source.shape[1]), BF),
        in_specs=[SMEM, VMEM, ANY],
        out_specs=VMEM,
        compiler_params=params(4),
        name="select",
    )(expert, source, after)


def stacked(refs, start, size):
    return jnp.concatenate([ref[:, start : start + size] for ref in refs], axis=0)


def low_high(rows):
    zeros = jnp.zeros_like(rows)
    return jnp.concatenate([rows, zeros], axis=0), jnp.concatenate([zeros, rows], axis=0)


def folded(weight, low, high):
    half = weight.shape[0] // 2
    return dot(weight[:half, :], low, 1, 1) + dot(weight[half:, :], high, 1, 1)


def first_kernel(count, position_ref, *refs):
    parts = refs[:count]
    w_gate, w_up, w_down, gate_out, up_out, through_out = refs[count:]
    width = w_gate.shape[0]
    here = pl.ds(pl.multiple_of(position_ref[0] * width, width), width)
    hidden = w_gate.shape[1]
    tile = min(512, hidden)
    inputs = stacked(parts, 0, width)
    upstream = stacked(parts, width, width)
    through_out[...] = folded(w_down.at[:, here], *low_high(upstream))
    for start in range(0, hidden, tile):
        units = slice(start, start + tile)
        gate_out[:, units] = dot(inputs, w_gate[:, units], 1, 0)
        up_out[:, units] = dot(inputs, w_up[here, units], 1, 0)


def second_kernel(count, others, position_ref, *refs):
    own = refs[:count]
    parts = [refs[count * (m + 1) : count * (m + 2)] for m in range(others)]
    rest = refs[count * (others + 1) :]
    w_gate, w_up, w_down, gate_in, up_in, through_in = rest[:6]
    weighted_ref, grad_gate_ref, grad_up_ref, inputs_ref, upstream_ref, routing_ref = rest[6:12]
    through_ref = rest[12]
    full = own[0].shape[1]
    width = (full - LANES) // 2
    position, expert = position_ref[0], position_ref[1]
    places = [pl.ds(pl.multiple_of((position ^ m) * width, width), width) for m in range(others + 1)]
    hidden = w_gate.shape[1]
    slots = gate_in.shape[0]
    half = hidden // 2
    tile = min(512, half)
    through = through_in[...]
    for m in range(others):
        upstream = stacked(parts[m], width, width)
        through = through + folded(w_down.at[:, places[m + 1]], *low_high(upstream))
    through_ref[...] = through.T
    info = stacked(own, full - LANES, LANES).astype(F32)
    lane = lax.broadcasted_iota(jnp.int32, info.shape, 1)
    scale = jnp.sum(jnp.where(lane == expert + E, info, 0.0), axis=1, keepdims=True)
    for m, blocks in enumerate([own] + parts):
        inputs_ref[:, places[m]] = stacked(blocks, 0, width)
        upstream_ref[:, places[m]] = stacked(blocks, width, width)
    xs = [stacked(part, 0, width) for part in parts]
    x = jnp.concatenate(xs, axis=1)
    score = jnp.zeros((slots, 1), F32)
    for start in range(0, hidden, tile):
        units = slice(start, start + tile)
        pre_gate = gate_in[:, units] + dot(x, w_gate[:, units], 1, 0)
        pre_up = up_in[:, units]
        for m in range(others):
            pre_up = pre_up + dot(xs[m], w_up[places[m + 1], units], 1, 0)
        side, offset = divmod(start, half)
        through = through_ref[side * slots : (side + 1) * slots, offset : offset + tile]
        sig = jax.nn.sigmoid(pre_gate)
        act = pre_gate * sig
        product = act * pre_up
        weighted_ref[:, units] = (scale * product).astype(BF)
        score = score + jnp.sum(through * product, axis=1, keepdims=True)
        scaled = scale * through
        grad_gate_ref[:, units] = (scaled * pre_up * sig * (1.0 + pre_gate * (1.0 - sig))).astype(BF)
        grad_up_ref[:, units] = (scaled * act).astype(BF)
    sub = lax.broadcasted_iota(jnp.int32, (slots, slots), 0)
    diagonal = lax.broadcasted_iota(jnp.int32, (slots, slots), 1)
    spread = jnp.where(sub == diagonal, jnp.broadcast_to(score, (slots, slots)), 0.0)
    routing_ref[...] = jnp.sum(spread, axis=0, keepdims=True)


def halves(row, rows):
    high = row.astype(BF).astype(F32)
    wide = jnp.concatenate([high, row - high], axis=1)
    sub = lax.broadcasted_iota(jnp.int32, (rows, wide.shape[1]), 0)
    return jnp.where(sub == 0, jnp.broadcast_to(wide, sub.shape), 0.0).astype(BF)


def back(position, mask, grad_gate, grad_up, w_gate, w_up, routing_ref, out_ref):
    width = w_gate.shape[0]
    half = width // 2

    def products(rows):
        part = folded(w_gate, *low_high(grad_gate[...])) + folded(w_up.at[rows], *low_high(grad_up[...]))
        out_ref[:half, :] = part.astype(out_ref.dtype)

    places = w_up.shape[0] // width
    if places == 2:
        for place in range(places):
            pl.when(position ^ mask == place)(functools.partial(products, pl.ds(place * width, width)))
    else:
        products(pl.ds(pl.multiple_of((position ^ mask) * width, width), width))
    if out_ref.shape[0] > half:
        out_ref[half:, :] = halves(routing_ref[...], out_ref.shape[0] - half)


def back_own_kernel(position_ref, *refs):
    back(position_ref[0], 0, *refs)


def back_other_kernel(others, position_ref, *refs):
    grad_gate, grad_up, w_gate, w_up, routing_ref = refs[:5]
    outs = refs[5:]
    width = w_gate.shape[0] // others
    for m, out_ref in enumerate(outs):
        rows = pl.ds(m * width, width)
        back(position_ref[0], m + 1, grad_gate, grad_up, w_gate.at[rows], w_up, routing_ref, out_ref)


def merge_kernel(after_ref, order_ref, own_ref, routing_ref, *refs):
    parts, out_ref = refs[:-1], refs[-1]
    half, lanes = own_ref.shape
    slots = lanes // 2
    total = own_ref[...]
    score = routing_ref[...]
    for part in parts:
        total = total + part[:half, :].astype(F32)
        tail = part[half : half + 1, :].astype(F32)
        score = score + tail[:, :slots] + tail[:, slots:]
    columns = jnp.concatenate([total.astype(BF), halves(score, out_ref.shape[1] - half)], axis=0)
    out_ref[...] = dot(order_ref[...], columns, 1, 1).astype(BF)


def plan_kernel(replicas, offsets, position_ref, experts_ref, after_ref, order_ref, *hit_refs):
    size = order_ref.shape[0]
    slots = size // 2
    out_row = lax.broadcasted_iota(jnp.int32, (size, size), 0)
    lane = lax.broadcasted_iota(jnp.int32, (size, size), 1)
    high = lane >= slots
    slot = jnp.where(high, lane - slots, lane)
    block = slot // CAP
    blocks = len(offsets)
    origin = jnp.zeros_like(slot)
    for r in range(replicas):
        for j, offset in enumerate(offsets):
            origin = jnp.where(block == r * blocks + j, offset ^ r, origin)
    origin = origin ^ position_ref[2]
    target = origin * (2 * CAP) + (slot - block * CAP) + jnp.where(high, CAP, 0)
    order_ref[...] = jnp.where(out_row == target, 1.0, 0.0).astype(BF)
    tok = experts_ref.shape[1]
    lane = lax.broadcasted_iota(jnp.int32, (tok, size), 1)
    lane_expert = (lane // (2 * CAP * replicas)).astype(F32)
    hit_first, hit_second, _, before = routing(experts_ref, lane_expert)
    here = before == (lane % CAP).astype(F32)
    low = lane % (2 * CAP) < CAP
    any_hit = (hit_first | hit_second) & here
    for ref, hit in zip(hit_refs, (any_hit & low, any_hit & ~low, hit_first & here, hit_second & here)):
        ref[...] = jnp.where(hit, 1.0, 0.0).astype(BF)


def finish_kernel(back_ref, low_ref, high_ref, first_ref, second_ref, grad_ref, routing_ref):
    tok, width = grad_ref.shape
    half = width // 2
    grad_ref[:, :half] = dot(low_ref[...], back_ref[:, :half], 1, 0).astype(BF)
    grad_ref[:, half:] = dot(high_ref[...], back_ref[:, :half], 1, 0).astype(BF)
    sub = lax.broadcasted_iota(jnp.int32, (tok, tok), 0)
    diagonal = lax.broadcasted_iota(jnp.int32, (tok, tok), 1)
    for k, ref in enumerate((first_ref, second_ref)):
        score = dot(ref[...], back_ref[:, half : half + LANES], 1, 0)[:, :1]
        spread = jnp.where(sub == diagonal, jnp.broadcast_to(score, (tok, tok)), 0.0)
        routing_ref[k : k + 1, :] = jnp.sum(spread, axis=0, keepdims=True)


def outer_kernel(tile, depth, count, *refs):
    lefts, rights, outs = refs[:count], refs[count : 2 * count], refs[2 * count : 3 * count]
    buffer, turned, sems = refs[3 * count :]
    steps = []
    for left, right, out in zip(lefts, rights, outs):
        rows, columns = out.shape
        steps += [(left, right, out, start) for start in range(0, rows, tile)]
    copies = []
    for i, (left, right, out, start) in enumerate(steps):
        slot = i % depth
        if start == 0:
            turned[: out.shape[0], :] = left[...].T
        if i >= depth:
            copies[i - depth].wait()
        columns = out.shape[1]
        place = buffer.at[slot, :, pl.ds(0, columns)]
        place[...] = dot(turned[start : start + tile, :], right[...], 1, 0).astype(BF)
        copies.append(pltpu.make_async_copy(place, out.at[pl.ds(start, tile)], sems.at[slot]))
        copies[i].start()
    for copy in copies[max(0, len(copies) - depth) :]:
        copy.wait()


def outer(pairs, name, weight=1):
    shapes = [(left.shape[1], right.shape[1]) for left, right in pairs]
    tile = min([512] + [rows for rows, _ in shapes])
    tile = next(size for size in (tile, 384, 256, 128) if all(rows % size == 0 for rows, _ in shapes))
    slots = pairs[0][0].shape[0]
    depth = 4
    widest = max(columns for _, columns in shapes)
    tallest = max(rows for rows, _ in shapes)
    size = sum(rows * columns for rows, columns in shapes)
    return pl.pallas_call(
        functools.partial(outer_kernel, tile, depth, len(pairs)),
        out_shape=[jax.ShapeDtypeStruct(shape, BF) for shape in shapes],
        in_specs=[VMEM] * (2 * len(pairs)),
        out_specs=[ANY] * len(pairs),
        scratch_shapes=[
            pltpu.VMEM((depth, tile, widest), BF),
            pltpu.VMEM((tallest, slots), BF),
            pltpu.SemaphoreType.DMA((depth,)),
        ],
        compiler_params=params(20),
        cost_estimate=cost(8 * slots * size // weight, 2 * size // weight),
        name=name,
    )(*[left for left, _ in pairs], *[right for _, right in pairs])


def shards(n_wide, n_tensor, tokens, cotangent, gates, experts, w_gate, w_up, w_down):
    axes = ("tensor", "wide")
    replicas = n_wide // E
    wide, tensor = lax.axis_index("wide"), lax.axis_index("tensor")
    tok, width = tokens.shape
    hidden = w_gate.shape[2]
    full = 2 * width + LANES
    slots = n_wide * CAP
    position = jnp.stack([tensor, wide // replicas, wide]).astype(jnp.int32)
    expert = (wide // replicas).astype(jnp.int32)[None]

    def swap(value, wide_mask, tensor_mask):
        pairs = [
            (t * n_wide + w, (t ^ tensor_mask) * n_wide + (w ^ wide_mask))
            for t in range(n_tensor)
            for w in range(n_wide)
        ]
        return lax.ppermute(value, axes, pairs)

    def shape(rows, columns, dtype=BF):
        return jax.ShapeDtypeStruct((rows, columns), dtype)

    experts_t = experts.T
    own = (0,)
    rest = tuple(range(1, n_tensor))
    gathered = pl.pallas_call(
        pack_kernel,
        out_shape=pltpu.VMEM((tok, full), BF),
        in_specs=[ANY] * 4,
        out_specs=VMEM,
        scratch_shapes=[
            pltpu.VMEM((2, tok), BF),
            pltpu.VMEM((2, tok), jnp.int32),
            pltpu.SemaphoreType.DMA((4,)),
        ],
        compiler_params=params(1),
        name="pack",
    )(*[pltpu.with_memory_space_constraint(x, pltpu.HBM) for x in (tokens, cotangent, gates.T, experts_t)])

    gate = w_gate[0]
    up, down = [pltpu.with_memory_space_constraint(w[0], pltpu.VMEM) for w in (w_up, w_down)]
    plan = [[(gate, True, own)], [(gate, True, rest)]]
    staged = []
    offsets = [0]
    mask = n_wide // 2
    while mask >= replicas:
        last = mask == replicas
        got = swap(gathered, mask, 0)
        jobs = sum(plan if last else plan[:1], [])
        plan = plan[1:]
        tokens_done = []
        if jobs:
            kept, token = stage(position, jobs, width, gathered)
            staged += kept
            tokens_done = [token]
        if not last:
            gathered = pl.pallas_call(
                join_kernel,
                out_shape=pltpu.VMEM((2 * gathered.shape[0], full), BF),
                in_specs=[VMEM] * 2 + [ANY] * len(tokens_done),
                out_specs=VMEM,
                compiler_params=params(2),
        name="join",
            )(gathered, got, *tokens_done)
        else:
            early = select(expert, gathered, len(offsets), position)
            every = offsets + [offset ^ mask for offset in offsets]
            order, *hits = pl.pallas_call(
                functools.partial(plan_kernel, replicas, every),
                out_shape=[pltpu.VMEM((2 * slots, 2 * slots), BF)] + [pltpu.VMEM((tok, 2 * slots), BF)] * 4,
                in_specs=[SMEM, VMEM, ANY],
                out_specs=[VMEM] * 5,
                compiler_params=params(4),
                name="plan",
            )(position, experts_t, early)
            late = select(expert, got, len(offsets), order)
        offsets = offsets + [offset ^ mask for offset in offsets]
        mask //= 2

    wg_own, wg_rest = staged
    pieces = [early, late]
    away = [[swap(piece, 0, m) for piece in pieces] for m in rest]
    near = pieces + [swap(piece, r, 0) for r in range(1, replicas) for piece in pieces]

    others = n_tensor - 1
    partial = pl.pallas_call(
        functools.partial(first_kernel, len(near)),
        out_shape=[shape(slots, hidden, F32)] * 2 + [shape(hidden // 2, 2 * slots, F32)],
        in_specs=[SMEM] + [VMEM] * (len(near) + 3),
        out_specs=[VMEM] * 3,
        compiler_params=params(5),
        cost_estimate=cost(24 * slots * width * hidden, 6 * width * hidden),
        name="first",
    )(position, *near, wg_own, up, down)

    parts = []
    for first_piece, second_piece in away:
        both = [first_piece, relay(second_piece, partial[0])]
        parts.append(both + [swap(piece, r, 0) for r in range(1, replicas) for piece in both])
    count = len(near)
    weighted, grad_gate, grad_up, inputs, upstream, score = pl.pallas_call(
        functools.partial(second_kernel, count, others),
        out_shape=[shape(slots, hidden)] * 3
        + [shape(slots, width * n_tensor)] * 2
        + [shape(1, slots, F32)],
        in_specs=[SMEM] + [VMEM] * (count * n_tensor + 6),
        out_specs=[VMEM] * 6,
        scratch_shapes=[pltpu.VMEM((2 * slots, hidden // 2), F32)],
        compiler_params=params(6),
        cost_estimate=cost(24 * slots * width * hidden, 6 * width * hidden),
        name="second",
    )(position, *near, *sum(parts, []), wg_rest, up, down, *partial)

    half = width // 2
    sent = pl.pallas_call(
        functools.partial(back_other_kernel, others),
        out_shape=[shape(half + 16, 2 * slots)] * others,
        in_specs=[SMEM] + [VMEM] * 5,
        out_specs=[VMEM] * others,
        compiler_params=params(5),
        cost_estimate=cost(16 * slots * width * hidden, 4 * width * hidden),
        name="back_other",
    )(position, grad_gate, grad_up, wg_rest, up, score)
    returned = [swap(value, 0, m) for m, value in zip(rest, sent)]
    kept = pl.pallas_call(
        back_own_kernel,
        out_shape=shape(half, 2 * slots, F32),
        in_specs=[SMEM] + [VMEM] * 5,
        out_specs=VMEM,
        compiler_params=params(5),
        cost_estimate=cost(16 * slots * width * hidden, 4 * width * hidden),
        name="back_own",
    )(position, grad_gate, grad_up, wg_own, up, score)
    (gate_proj_grad,) = outer([(inputs, grad_gate)], "gate_grad", 16)
    merged = pl.pallas_call(
        merge_kernel,
        out_shape=shape(2 * slots, half + LANES),
        in_specs=[ANY] + [VMEM] * (3 + others),
        out_specs=VMEM,
        compiler_params=params(4),
        name="merge",
    )(pltpu.with_memory_space_constraint(gate_proj_grad, pltpu.HBM), order, kept, score, *returned)
    landed = lax.all_to_all(merged, "wide", split_axis=0, concat_axis=0, tiled=True)
    up_proj_grad, down_proj_grad = outer([(inputs, grad_up), (weighted, upstream)], "other_grads")
    input_grad, routing_grad = pl.pallas_call(
        finish_kernel,
        out_shape=[shape(tok, width), shape(2, tok, F32)],
        in_specs=[VMEM] * 5,
        out_specs=[VMEM] * 2,
        compiler_params=params(3),
        name="finish",
    )(landed, *hits)
    return (
        input_grad,
        routing_grad.T,
        gate_proj_grad[None],
        up_proj_grad[None],
        down_proj_grad[None],
    )


def solution(mesh):
    return jax.shard_map(
        functools.partial(shards, mesh.shape["wide"], mesh.shape["tensor"]),
        mesh=mesh,
        in_specs=(
            P("wide", "tensor"),
            P("wide", "tensor"),
            P("wide", None),
            P("wide", None),
            P("wide", None, "tensor"),
            P("wide", None, "tensor"),
            P("wide", "tensor", None),
        ),
        out_specs=(
            P("wide", "tensor"),
            P("wide", None),
            P("wide", None, "tensor"),
            P("wide", None, "tensor"),
            P("wide", "tensor", None),
        ),
        check_vma=False,
    )
```

```python
import functools

import jax
import jax.numpy as jnp
from jax import lax
from jax.experimental import pallas as pl
from jax.experimental.pallas import tpu as pltpu
from jax.sharding import PartitionSpec as P

E = 8
CAP = 4
LANES = 128
BF = jnp.bfloat16
F32 = jnp.float32
VMEM = pl.BlockSpec(memory_space=pltpu.VMEM)
SMEM = pl.BlockSpec(memory_space=pltpu.SMEM)
ANY = pl.BlockSpec(memory_space=pl.ANY)


def dot(left, right, left_dim, right_dim):
    return lax.dot_general(
        left, right, (((left_dim,), (right_dim,)), ((), ())), preferred_element_type=F32
    )


def params(mib):
    return pltpu.CompilerParams(vmem_limit_bytes=mib << 20)


def cost(flops, moved):
    return pl.CostEstimate(flops=flops, bytes_accessed=moved, transcendentals=0)


def column(row):
    n = row.shape[1]
    sub = lax.broadcasted_iota(jnp.int32, (n, n), 0)
    lane = lax.broadcasted_iota(jnp.int32, (n, n), 1)
    return jnp.sum(jnp.where(sub == lane, jnp.broadcast_to(row, (n, n)), 0.0), axis=1, keepdims=True)


def routing(experts_ref, lane_expert):
    ids = experts_ref[...].astype(F32)
    first, second = column(ids[0:1, :]), column(ids[1:2, :])
    hit_first = lane_expert == first
    hit_second = lane_expert == second
    picked = jnp.where(hit_first | hit_second, 1.0, 0.0)
    sub = lax.broadcasted_iota(jnp.int32, picked.shape, 0)
    before = jnp.zeros_like(picked)
    for row in range(picked.shape[0] - 1):
        before = before + jnp.where(sub > row, picked[row : row + 1, :], 0.0)
    return hit_first, hit_second, picked, before


def pack_kernel(
    tokens_hbm, cotangent_hbm, gates_hbm, experts_hbm, out_ref, gates_ref, experts_ref, sems
):
    rows, width = tokens_hbm.shape
    copies = [
        pltpu.make_async_copy(source, target, sems.at[i])
        for i, (source, target) in enumerate(
            (
                (gates_hbm, gates_ref),
                (experts_hbm, experts_ref),
                (tokens_hbm, out_ref.at[:, pl.ds(0, width)]),
                (cotangent_hbm, out_ref.at[:, pl.ds(width, width)]),
            )
        )
    ]
    for copy in copies:
        copy.start()
    copies[0].wait()
    copies[1].wait()
    lane = lax.broadcasted_iota(jnp.int32, (rows, LANES), 1)
    lane_expert = (lane % E).astype(F32)
    hit_first, hit_second, picked, before = routing(experts_ref, lane_expert)
    gates = gates_ref[...].astype(F32)
    gate = jnp.where(hit_first, column(gates[0:1, :]), 0.0) + jnp.where(
        hit_second, column(gates[1:2, :]), 0.0
    )
    place = jnp.where(picked > 0.5, before, -1.0)
    info = jnp.where(lane < E, place, jnp.where(lane < 2 * E, gate, 0.0))
    out_ref[:, 2 * width :] = info.astype(BF)
    copies[2].wait()
    copies[3].wait()


def part_copies(position, by_row, masks, source, target, sems):
    copies = []
    for i, mask in enumerate(masks):
        if by_row:
            width = target.shape[0] // len(masks)
            place = pl.ds(pl.multiple_of((position ^ mask) * width, width), width)
            pair = (source.at[place], target.at[pl.ds(i * width, width)])
        else:
            width = target.shape[1]
            depth = target.shape[0] // len(masks)
            place = pl.ds(pl.multiple_of((position ^ mask) * width, width), width)
            pair = (source.at[:, place], target.at[pl.ds(i * depth, depth)])
        copies.append(pltpu.make_async_copy(*pair, sems.at[i]))
    return copies


def part_shape(weight, by_row, masks, width):
    if by_row:
        return pltpu.VMEM((width * len(masks), weight.shape[1]), BF)
    return pltpu.VMEM((weight.shape[0] * len(masks), width), BF)


def stage_kernel(jobs, position_ref, after_ref, *refs):
    count = len(jobs)
    sources, outs = refs[:count], refs[count : 2 * count]
    token_ref = refs[2 * count]
    copies = []
    for (by_row, masks), source, out, sems in zip(jobs, sources, outs, refs[2 * count + 1 :]):
        copies += part_copies(position_ref[0], by_row, masks, source, out, sems)
    for copy in copies:
        copy.start()
    token_ref[...] = jnp.zeros_like(token_ref)
    for copy in copies:
        copy.wait()


def stage(position, jobs, width, after):
    outs = [part_shape(*job, width) for job in jobs]
    size = sum(out.shape[0] * out.shape[1] for out in outs)
    *kept, token = pl.pallas_call(
        functools.partial(stage_kernel, [job[1:] for job in jobs]),
        out_shape=outs + [pltpu.VMEM((8, LANES), F32)],
        in_specs=[SMEM, ANY] + [ANY] * len(jobs),
        out_specs=[ANY] * len(jobs) + [VMEM],
        scratch_shapes=[pltpu.SemaphoreType.DMA((len(job[2]),)) for job in jobs],
        compiler_params=params(2),
        cost_estimate=cost(0, 4 * size),
        name="stage",
    )(position, after, *[pltpu.with_memory_space_constraint(job[0], pltpu.HBM) for job in jobs])
    return kept, token


def join_kernel(own_ref, got_ref, *refs):
    out_ref = refs[-1]
    rows = own_ref.shape[0]
    out_ref[:rows, :] = own_ref[...]
    out_ref[rows:, :] = got_ref[...]


def join(first, second, after):
    return pl.pallas_call(
        join_kernel,
        out_shape=pltpu.VMEM((first.shape[0] + second.shape[0], first.shape[1]), BF),
        in_specs=[VMEM, VMEM, ANY],
        out_specs=VMEM,
        compiler_params=params(2),
        name="join",
    )(first, second, after)


def select_kernel(expert_ref, source_ref, *refs):
    out_ref = refs[-1]
    tok_rows, full = source_ref.shape
    slots = out_ref.shape[0]
    per_block = tok_rows // (slots // CAP)
    info = source_ref[:, full - LANES :].astype(F32)
    lane = lax.broadcasted_iota(jnp.int32, info.shape, 1)
    place = jnp.sum(jnp.where(lane == expert_ref[0], info, 0.0), axis=1, keepdims=True)
    row = lax.broadcasted_iota(jnp.int32, (tok_rows, slots), 0)
    col = lax.broadcasted_iota(jnp.int32, (tok_rows, slots), 1)
    take = (row // per_block == col // CAP) & (place == (col % CAP).astype(F32))
    out_ref[...] = dot(jnp.where(take, 1.0, 0.0).astype(BF), source_ref[...], 0, 0).astype(BF)


def select(expert, source, blocks, after):
    return pl.pallas_call(
        select_kernel,
        out_shape=pltpu.VMEM((blocks * CAP, source.shape[1]), BF),
        in_specs=[SMEM, VMEM, ANY],
        out_specs=VMEM,
        compiler_params=params(4),
        name="select",
    )(expert, source, after)


def stacked(refs, start, size):
    return jnp.concatenate([ref[:, start : start + size] for ref in refs], axis=0)


def low_high(rows):
    zeros = jnp.zeros_like(rows)
    return jnp.concatenate([rows, zeros], axis=0), jnp.concatenate([zeros, rows], axis=0)


def folded(weight, low, high):
    half = weight.shape[0] // 2
    return dot(weight[:half, :], low, 1, 1) + dot(weight[half:, :], high, 1, 1)


def first_kernel(count, position_ref, *refs):
    parts = refs[:count]
    w_gate, w_up, w_down, gate_out, up_out, through_out = refs[count:]
    width = w_gate.shape[0]
    here = pl.ds(pl.multiple_of(position_ref[0] * width, width), width)
    hidden = w_gate.shape[1]
    tile = min(512, hidden)
    inputs = stacked(parts, 0, width)
    upstream = stacked(parts, width, width)
    through_out[...] = folded(w_down.at[:, here], *low_high(upstream))
    for start in range(0, hidden, tile):
        units = slice(start, start + tile)
        gate_out[:, units] = dot(inputs, w_gate[:, units], 1, 0)
        up_out[:, units] = dot(inputs, w_up[here, units], 1, 0)


def second_kernel(count, others, position_ref, *refs):
    own = refs[:count]
    parts = [refs[count * (m + 1) : count * (m + 2)] for m in range(others)]
    rest = refs[count * (others + 1) :]
    w_gate, w_up, w_down, gate_in, up_in, through_in = rest[:6]
    weighted_ref, grad_gate_ref, grad_up_ref, inputs_ref, upstream_ref, routing_ref = rest[6:12]
    through_ref = rest[12]
    full = own[0].shape[1]
    width = (full - LANES) // 2
    position, expert = position_ref[0], position_ref[1]
    places = [pl.ds(pl.multiple_of((position ^ m) * width, width), width) for m in range(others + 1)]
    hidden = w_gate.shape[1]
    slots = gate_in.shape[0]
    half = hidden // 2
    tile = min(512, half)
    through = through_in[...]
    for m in range(others):
        upstream = stacked(parts[m], width, width)
        through = through + folded(w_down.at[:, places[m + 1]], *low_high(upstream))
    through_ref[...] = through.T
    info = stacked(own, full - LANES, LANES).astype(F32)
    lane = lax.broadcasted_iota(jnp.int32, info.shape, 1)
    scale = jnp.sum(jnp.where(lane == expert + E, info, 0.0), axis=1, keepdims=True)
    for m, blocks in enumerate([own] + parts):
        inputs_ref[:, places[m]] = stacked(blocks, 0, width)
        upstream_ref[:, places[m]] = stacked(blocks, width, width)
    xs = [stacked(part, 0, width) for part in parts]
    x = jnp.concatenate(xs, axis=1)
    score = jnp.zeros((slots, 1), F32)
    for start in range(0, hidden, tile):
        units = slice(start, start + tile)
        pre_gate = gate_in[:, units] + dot(x, w_gate[:, units], 1, 0)
        pre_up = up_in[:, units]
        for m in range(others):
            pre_up = pre_up + dot(xs[m], w_up[places[m + 1], units], 1, 0)
        side, offset = divmod(start, half)
        through = through_ref[side * slots : (side + 1) * slots, offset : offset + tile]
        sig = jax.nn.sigmoid(pre_gate)
        act = pre_gate * sig
        product = act * pre_up
        weighted_ref[:, units] = (scale * product).astype(BF)
        score = score + jnp.sum(through * product, axis=1, keepdims=True)
        scaled = scale * through
        grad_gate_ref[:, units] = (scaled * pre_up * sig * (1.0 + pre_gate * (1.0 - sig))).astype(BF)
        grad_up_ref[:, units] = (scaled * act).astype(BF)
    sub = lax.broadcasted_iota(jnp.int32, (slots, slots), 0)
    diagonal = lax.broadcasted_iota(jnp.int32, (slots, slots), 1)
    spread = jnp.where(sub == diagonal, jnp.broadcast_to(score, (slots, slots)), 0.0)
    routing_ref[...] = jnp.sum(spread, axis=0, keepdims=True)


def halves(row, rows):
    high = row.astype(BF).astype(F32)
    wide = jnp.concatenate([high, row - high], axis=1)
    sub = lax.broadcasted_iota(jnp.int32, (rows, wide.shape[1]), 0)
    return jnp.where(sub == 0, jnp.broadcast_to(wide, sub.shape), 0.0).astype(BF)


def back(position, mask, grad_gate, grad_up, w_gate, w_up, routing_ref, out_ref):
    width = w_gate.shape[0]
    half = width // 2

    gate_rows, up_rows = low_high(grad_gate[...]), low_high(grad_up[...])

    rows = pl.ds(pl.multiple_of((position ^ mask) * width, width), width)
    part = folded(w_gate, *gate_rows) + folded(w_up.at[rows], *up_rows)
    out_ref[:half, :] = part.astype(out_ref.dtype)
    if out_ref.shape[0] > half:
        out_ref[half:, :] = halves(routing_ref[...], out_ref.shape[0] - half)


def back_other_kernel(others, position_ref, *refs):
    grad_gate, grad_up, w_gate, w_up, routing_ref = refs[:5]
    outs = refs[5:]
    width = w_gate.shape[0] // others
    for m, out_ref in enumerate(outs):
        rows = pl.ds(m * width, width)
        back(position_ref[0], m + 1, grad_gate, grad_up, w_gate.at[rows], w_up, routing_ref, out_ref)


def merge_kernel(order_ref, own_ref, routing_ref, *refs):
    parts, out_ref = refs[:-1], refs[-1]
    half, lanes = own_ref.shape
    slots = lanes // 2
    total = own_ref[...]
    score = routing_ref[...]
    for part in parts:
        total = total + part[:half, :].astype(F32)
        tail = part[half : half + 1, :].astype(F32)
        score = score + tail[:, :slots] + tail[:, slots:]
    columns = jnp.concatenate([total.astype(BF), halves(score, out_ref.shape[1] - half)], axis=0)
    out_ref[...] = dot(order_ref[...], columns, 1, 1).astype(BF)


def plan_kernel(replicas, offsets, position_ref, experts_ref, after_ref, order_ref, *hit_refs):
    size = order_ref.shape[0]
    slots = size // 2
    out_row = lax.broadcasted_iota(jnp.int32, (size, size), 0)
    lane = lax.broadcasted_iota(jnp.int32, (size, size), 1)
    high = lane >= slots
    slot = jnp.where(high, lane - slots, lane)
    block = slot // CAP
    blocks = len(offsets)
    origin = jnp.zeros_like(slot)
    for r in range(replicas):
        for j, offset in enumerate(offsets):
            origin = jnp.where(block == r * blocks + j, offset ^ r, origin)
    origin = origin ^ position_ref[2]
    target = origin * (2 * CAP) + (slot - block * CAP) + jnp.where(high, CAP, 0)
    order_ref[...] = jnp.where(out_row == target, 1.0, 0.0).astype(BF)
    tok = experts_ref.shape[1]
    lane = lax.broadcasted_iota(jnp.int32, (tok, size), 1)
    lane_expert = (lane // (2 * CAP * replicas)).astype(F32)
    hit_first, hit_second, _, before = routing(experts_ref, lane_expert)
    here = before == (lane % CAP).astype(F32)
    low = lane % (2 * CAP) < CAP
    any_hit = (hit_first | hit_second) & here
    for ref, hit in zip(hit_refs, (any_hit & low, any_hit & ~low, hit_first & here, hit_second & here)):
        ref[...] = jnp.where(hit, 1.0, 0.0).astype(BF)


def finish_kernel(back_ref, low_ref, high_ref, first_ref, second_ref, grad_ref, routing_ref):
    tok, width = grad_ref.shape
    half = width // 2
    grad_ref[:, :half] = dot(low_ref[...], back_ref[:, :half], 1, 0).astype(BF)
    grad_ref[:, half:] = dot(high_ref[...], back_ref[:, :half], 1, 0).astype(BF)
    sub = lax.broadcasted_iota(jnp.int32, (tok, tok), 0)
    diagonal = lax.broadcasted_iota(jnp.int32, (tok, tok), 1)
    for k, ref in enumerate((first_ref, second_ref)):
        score = dot(ref[...], back_ref[:, half : half + LANES], 1, 0)[:, :1]
        spread = jnp.where(sub == diagonal, jnp.broadcast_to(score, (tok, tok)), 0.0)
        routing_ref[k : k + 1, :] = jnp.sum(spread, axis=0, keepdims=True)


def outer_kernel(tile, depth, count, *refs):
    lefts, rights, outs = refs[:count], refs[count : 2 * count], refs[2 * count : 3 * count]
    for copy in outer_copies(tile, depth, lefts, rights, outs, *refs[3 * count :]):
        copy.wait()


def outer_back_kernel(tile, depth, position_ref, left, right, grad_up, w_gate, w_up, score_ref, out, kept, *scratch):
    pending = outer_copies(tile, depth, [left], [right], [out], *scratch)
    back(position_ref[0], 0, right, grad_up, w_gate, w_up, score_ref, kept)
    for copy in pending:
        copy.wait()


def outer_copies(tile, depth, lefts, rights, outs, buffer, turned, sems):
    steps = []
    for left, right, out in zip(lefts, rights, outs):
        rows, columns = out.shape
        steps += [(left, right, out, start) for start in range(0, rows, tile)]
    copies = []
    for i, (left, right, out, start) in enumerate(steps):
        slot = i % depth
        if start == 0:
            turned[: out.shape[0], :] = left[...].T
        if i >= depth:
            copies[i - depth].wait()
        columns = out.shape[1]
        place = buffer.at[slot, :, pl.ds(0, columns)]
        place[...] = dot(turned[start : start + tile, :], right[...], 1, 0).astype(BF)
        copies.append(pltpu.make_async_copy(place, out.at[pl.ds(start, tile)], sems.at[slot]))
        copies[i].start()
    return copies[max(0, len(copies) - depth) :]


def outer_plan(shapes, slots):
    tile = min([512] + [rows for rows, _ in shapes])
    tile = next(size for size in (tile, 384, 256, 128) if all(rows % size == 0 for rows, _ in shapes))
    depth = 4
    widest = max(columns for _, columns in shapes)
    tallest = max(rows for rows, _ in shapes)
    scratch = [
        pltpu.VMEM((depth, tile, widest), BF),
        pltpu.VMEM((tallest, slots), BF),
        pltpu.SemaphoreType.DMA((depth,)),
    ]
    return tile, depth, scratch


def outer(pairs, name):
    shapes = [(left.shape[1], right.shape[1]) for left, right in pairs]
    slots = pairs[0][0].shape[0]
    tile, depth, scratch = outer_plan(shapes, slots)
    size = sum(rows * columns for rows, columns in shapes)
    return pl.pallas_call(
        functools.partial(outer_kernel, tile, depth, len(pairs)),
        out_shape=[jax.ShapeDtypeStruct(shape, BF) for shape in shapes],
        in_specs=[VMEM] * (2 * len(pairs)),
        out_specs=[ANY] * len(pairs),
        scratch_shapes=scratch,
        compiler_params=params(20),
        cost_estimate=cost(8 * slots * size, 2 * size),
        name=name,
    )(*[left for left, _ in pairs], *[right for _, right in pairs])


def shards(n_wide, n_tensor, tokens, cotangent, gates, experts, w_gate, w_up, w_down):
    axes = ("tensor", "wide")
    replicas = n_wide // E
    wide, tensor = lax.axis_index("wide"), lax.axis_index("tensor")
    tok, width = tokens.shape
    hidden = w_gate.shape[2]
    full = 2 * width + LANES
    slots = n_wide * CAP
    position = jnp.stack([tensor, wide // replicas, wide]).astype(jnp.int32)
    expert = (wide // replicas).astype(jnp.int32)[None]

    def swap(value, wide_mask, tensor_mask):
        pairs = [
            (t * n_wide + w, (t ^ tensor_mask) * n_wide + (w ^ wide_mask))
            for t in range(n_tensor)
            for w in range(n_wide)
        ]
        return lax.ppermute(value, axes, pairs)

    def shape(rows, columns, dtype=BF):
        return jax.ShapeDtypeStruct((rows, columns), dtype)

    experts_t = experts.T
    own = (0,)
    rest = tuple(range(1, n_tensor))
    gathered = pl.pallas_call(
        pack_kernel,
        out_shape=pltpu.VMEM((tok, full), BF),
        in_specs=[ANY] * 4,
        out_specs=VMEM,
        scratch_shapes=[
            pltpu.VMEM((2, tok), BF),
            pltpu.VMEM((2, tok), jnp.int32),
            pltpu.SemaphoreType.DMA((4,)),
        ],
        compiler_params=params(1),
        name="pack",
    )(*[pltpu.with_memory_space_constraint(x, pltpu.HBM) for x in (tokens, cotangent, gates.T, experts_t)])

    gate = w_gate[0]
    up, down = [pltpu.with_memory_space_constraint(w[0], pltpu.VMEM) for w in (w_up, w_down)]
    plan = [[(gate, True, own)], [(gate, True, rest)]]
    staged = []
    offsets = [0]
    mask = n_wide // 2
    while mask >= replicas:
        last = mask == replicas
        got = swap(gathered, mask, 0)
        jobs = sum(plan if last else plan[:1], [])
        plan = plan[1:]
        if jobs:
            kept, token = stage(position, jobs, width, gathered)
            staged += kept
        if not last:
            gathered = join(gathered, got, token if jobs else got)
        else:
            early = select(expert, gathered, len(offsets), position)
            every = offsets + [offset ^ mask for offset in offsets]
            order, *hits = pl.pallas_call(
                functools.partial(plan_kernel, replicas, every),
                out_shape=[pltpu.VMEM((2 * slots, 2 * slots), BF)] + [pltpu.VMEM((tok, 2 * slots), BF)] * 4,
                in_specs=[SMEM, VMEM, ANY],
                out_specs=[VMEM] * 5,
                compiler_params=params(4),
                name="plan",
            )(position, experts_t, early)
            late = select(expert, got, len(offsets), order)
        offsets = offsets + [offset ^ mask for offset in offsets]
        mask //= 2

    wg_own, wg_rest = staged
    away = [[swap(early, 0, m), swap(late, 0, m)] for m in rest]
    chosen = join(early, late, away[0][0])
    near = [chosen] + [swap(chosen, r, 0) for r in range(1, replicas)]

    others = n_tensor - 1
    partial = pl.pallas_call(
        functools.partial(first_kernel, len(near)),
        out_shape=[shape(slots, hidden, F32)] * 2 + [shape(hidden // 2, 2 * slots, F32)],
        in_specs=[SMEM] + [VMEM] * (len(near) + 3),
        out_specs=[VMEM] * 3,
        compiler_params=params(5),
        cost_estimate=cost(2 * slots * width * hidden, width * hidden // 2),
        name="first",
    )(position, *near, wg_own, up, down)

    parts = []
    for early_part, late_part in away:
        part = join(early_part, late_part, partial[0])
        parts.append([part] + [swap(part, r, 0) for r in range(1, replicas)])
    count = len(near)
    weighted, grad_gate, grad_up, inputs, upstream, score = pl.pallas_call(
        functools.partial(second_kernel, count, others),
        out_shape=[shape(slots, hidden)] * 3
        + [shape(slots, width * n_tensor)] * 2
        + [shape(1, slots, F32)],
        in_specs=[SMEM] + [VMEM] * (count * n_tensor + 6),
        out_specs=[VMEM] * 6,
        scratch_shapes=[pltpu.VMEM((2 * slots, hidden // 2), F32)],
        compiler_params=params(6),
        cost_estimate=cost(24 * slots * width * hidden, 6 * width * hidden),
        name="second",
    )(position, *near, *sum(parts, []), wg_rest, up, down, *partial)

    half = width // 2
    sent = pl.pallas_call(
        functools.partial(back_other_kernel, others),
        out_shape=[shape(half + 16, 2 * slots)] * others,
        in_specs=[SMEM] + [VMEM] * 5,
        out_specs=[VMEM] * others,
        compiler_params=params(5),
        cost_estimate=cost(16 * slots * width * hidden, 4 * width * hidden),
        name="back_other",
    )(position, grad_gate, grad_up, wg_rest, up, score)
    returned = [swap(value, 0, m) for m, value in zip(rest, sent)]
    grad_shape = (inputs.shape[1], hidden)
    tile, depth, scratch = outer_plan([grad_shape], slots)
    gate_proj_grad, kept = pl.pallas_call(
        functools.partial(outer_back_kernel, tile, depth),
        out_shape=[jax.ShapeDtypeStruct(grad_shape, BF), shape(half, 2 * slots, F32)],
        in_specs=[SMEM] + [VMEM] * 6,
        out_specs=[ANY, VMEM],
        scratch_shapes=scratch,
        compiler_params=params(16),
        cost_estimate=cost(8 * slots * grad_shape[0] * hidden, 2 * grad_shape[0] * hidden),
        name="gate_grad",
    )(position, inputs, grad_gate, grad_up, wg_own, up, score)
    merged = pl.pallas_call(
        merge_kernel,
        out_shape=shape(2 * slots, half + LANES),
        in_specs=[VMEM] * (3 + others),
        out_specs=VMEM,
        compiler_params=params(4),
        name="merge",
    )(order, kept, score, *returned)
    landed = lax.all_to_all(merged, "wide", split_axis=0, concat_axis=0, tiled=True)
    up_proj_grad, down_proj_grad = outer([(inputs, grad_up), (weighted, upstream)], "other_grads")
    input_grad, routing_grad = pl.pallas_call(
        finish_kernel,
        out_shape=[shape(tok, width), shape(2, tok, F32)],
        in_specs=[VMEM] * 5,
        out_specs=[VMEM] * 2,
        compiler_params=params(3),
        name="finish",
    )(landed, *hits)
    return (
        input_grad,
        routing_grad.T,
        gate_proj_grad[None],
        up_proj_grad[None],
        down_proj_grad[None],
    )


def solution(mesh):
    return jax.shard_map(
        functools.partial(shards, mesh.shape["wide"], mesh.shape["tensor"]),
        mesh=mesh,
        in_specs=(
            P("wide", "tensor"),
            P("wide", "tensor"),
            P("wide", None),
            P("wide", None),
            P("wide", None, "tensor"),
            P("wide", None, "tensor"),
            P("wide", "tensor", None),
        ),
        out_specs=(
            P("wide", "tensor"),
            P("wide", None),
            P("wide", None, "tensor"),
            P("wide", None, "tensor"),
            P("wide", "tensor", None),
        ),
        check_vma=False,
    )
```

```python
import functools

import jax
import jax.numpy as jnp
from jax import lax
from jax.experimental import pallas as pl
from jax.experimental.pallas import tpu as pltpu
from jax.sharding import PartitionSpec as P

E = 8
CAP = 4
LANES = 128
BF = jnp.bfloat16
F32 = jnp.float32
VMEM = pl.BlockSpec(memory_space=pltpu.VMEM)
SMEM = pl.BlockSpec(memory_space=pltpu.SMEM)
ANY = pl.BlockSpec(memory_space=pl.ANY)


def dot(left, right, left_dim, right_dim):
    return lax.dot_general(
        left, right, (((left_dim,), (right_dim,)), ((), ())), preferred_element_type=F32
    )


def params(mib):
    return pltpu.CompilerParams(vmem_limit_bytes=mib << 20)


def cost(flops, moved):
    return pl.CostEstimate(flops=flops, bytes_accessed=moved, transcendentals=0)


def column(row):
    n = row.shape[1]
    sub = lax.broadcasted_iota(jnp.int32, (n, n), 0)
    lane = lax.broadcasted_iota(jnp.int32, (n, n), 1)
    return jnp.sum(jnp.where(sub == lane, jnp.broadcast_to(row, (n, n)), 0.0), axis=1, keepdims=True)


def routing(experts_ref, lane_expert):
    ids = experts_ref[...].astype(F32)
    first, second = column(ids[0:1, :]), column(ids[1:2, :])
    hit_first = lane_expert == first
    hit_second = lane_expert == second
    picked = jnp.where(hit_first | hit_second, 1.0, 0.0)
    sub = lax.broadcasted_iota(jnp.int32, picked.shape, 0)
    before = jnp.zeros_like(picked)
    for row in range(picked.shape[0] - 1):
        before = before + jnp.where(sub > row, picked[row : row + 1, :], 0.0)
    return hit_first, hit_second, picked, before


def pack_kernel(
    tokens_hbm, cotangent_hbm, gates_hbm, experts_hbm, out_ref, gates_ref, experts_ref, sems
):
    rows, width = tokens_hbm.shape
    copies = [
        pltpu.make_async_copy(source, target, sems.at[i])
        for i, (source, target) in enumerate(
            (
                (gates_hbm, gates_ref),
                (experts_hbm, experts_ref),
                (tokens_hbm, out_ref.at[:, pl.ds(0, width)]),
                (cotangent_hbm, out_ref.at[:, pl.ds(width, width)]),
            )
        )
    ]
    for copy in copies:
        copy.start()
    copies[0].wait()
    copies[1].wait()
    lane = lax.broadcasted_iota(jnp.int32, (rows, LANES), 1)
    lane_expert = (lane % E).astype(F32)
    hit_first, hit_second, picked, before = routing(experts_ref, lane_expert)
    gates = gates_ref[...].astype(F32)
    gate = jnp.where(hit_first, column(gates[0:1, :]), 0.0) + jnp.where(
        hit_second, column(gates[1:2, :]), 0.0
    )
    place = jnp.where(picked > 0.5, before, -1.0)
    info = jnp.where(lane < E, place, jnp.where(lane < 2 * E, gate, 0.0))
    out_ref[:, 2 * width :] = info.astype(BF)
    copies[2].wait()
    copies[3].wait()


def part_copies(position, masks, width, offset, source, target, sems):
    rows = target.shape[0] // len(masks)
    copies = []
    for i, mask in enumerate(masks):
        start = pl.multiple_of((position ^ mask) * width + offset, rows)
        place = target.at[pl.ds(i * rows, rows)]
        copies.append(pltpu.make_async_copy(source.at[pl.ds(start, rows)], place, sems.at[i]))
    return copies


def stage_kernel(masks, width, offset, position_ref, after_ref, source_ref, out_ref, token_ref, sems):
    copies = part_copies(position_ref[0], masks, width, offset, source_ref, out_ref, sems)
    for copy in copies:
        copy.start()
    token_ref[...] = jnp.zeros_like(token_ref)
    for copy in copies:
        copy.wait()


def stage(position, weight, masks, width, offset, rows, after):
    columns = weight.shape[1]
    return pl.pallas_call(
        functools.partial(stage_kernel, masks, width, offset),
        out_shape=[pltpu.VMEM((rows * len(masks), columns), BF), pltpu.VMEM((8, LANES), F32)],
        in_specs=[SMEM, ANY, ANY],
        out_specs=[ANY, VMEM],
        scratch_shapes=[pltpu.SemaphoreType.DMA((len(masks),))],
        compiler_params=params(2),
        cost_estimate=cost(0, 4 * rows * len(masks) * columns),
        name="stage",
    )(position, after, pltpu.with_memory_space_constraint(weight, pltpu.HBM))


def join_kernel(own_ref, got_ref, *refs):
    out_ref = refs[-1]
    rows = own_ref.shape[0]
    out_ref[:rows, :] = own_ref[...]
    out_ref[rows:, :] = got_ref[...]


def join(first, second, after):
    return pl.pallas_call(
        join_kernel,
        out_shape=pltpu.VMEM((first.shape[0] + second.shape[0], first.shape[1]), BF),
        in_specs=[VMEM, VMEM, ANY],
        out_specs=VMEM,
        compiler_params=params(2),
        name="join",
    )(first, second, after)


def select_kernel(expert_ref, source_ref, *refs):
    out_ref = refs[-1]
    tok_rows, full = source_ref.shape
    slots = out_ref.shape[0]
    per_block = tok_rows // (slots // CAP)
    info = source_ref[:, full - LANES :].astype(F32)
    lane = lax.broadcasted_iota(jnp.int32, info.shape, 1)
    place = jnp.sum(jnp.where(lane == expert_ref[0], info, 0.0), axis=1, keepdims=True)
    row = lax.broadcasted_iota(jnp.int32, (tok_rows, slots), 0)
    col = lax.broadcasted_iota(jnp.int32, (tok_rows, slots), 1)
    take = (row // per_block == col // CAP) & (place == (col % CAP).astype(F32))
    out_ref[...] = dot(jnp.where(take, 1.0, 0.0).astype(BF), source_ref[...], 0, 0).astype(BF)


def select(expert, source, blocks, *after):
    return pl.pallas_call(
        select_kernel,
        out_shape=pltpu.VMEM((blocks * CAP, source.shape[1]), BF),
        in_specs=[SMEM, VMEM] + [ANY] * len(after),
        out_specs=VMEM,
        compiler_params=params(4),
        name="select",
    )(expert, source, *after)


def stacked(refs, start, size):
    return jnp.concatenate([ref[:, start : start + size] for ref in refs], axis=0)


def low_high(rows):
    zeros = jnp.zeros_like(rows)
    return jnp.concatenate([rows, zeros], axis=0), jnp.concatenate([zeros, rows], axis=0)


def folded(weight, low, high):
    half = weight.shape[0] // 2
    return dot(weight[:half, :], low, 1, 1) + dot(weight[half:, :], high, 1, 1)


def first_kernel(count, position_ref, *refs):
    parts = refs[:count]
    w_gate, w_up, w_down, gate_out, up_out, through_out = refs[count:]
    width = w_gate.shape[0]
    here = pl.ds(pl.multiple_of(position_ref[0] * width, width), width)
    hidden = w_gate.shape[1]
    tile = min(512, hidden)
    inputs = stacked(parts, 0, width)
    upstream = stacked(parts, width, width)
    through_out[...] = folded(w_down.at[:, here], *low_high(upstream))
    for start in range(0, hidden, tile):
        units = slice(start, start + tile)
        gate_out[:, units] = dot(inputs, w_gate[:, units], 1, 0)
        up_out[:, units] = dot(inputs, w_up[here, units], 1, 0)


def second_kernel(count, others, position_ref, after_ref, *refs):
    own = refs[:count]
    parts = [refs[count * (m + 1) : count * (m + 2)] for m in range(others)]
    rest = refs[count * (others + 1) :]
    w_low, w_high, w_up, w_down, gate_in, up_in, through_in = rest[:7]
    weighted_ref, grad_gate_ref, grad_up_ref, inputs_ref, upstream_ref, routing_ref = rest[7:13]
    through_ref = rest[13]
    full = own[0].shape[1]
    width = (full - LANES) // 2
    position, expert = position_ref[0], position_ref[1]
    places = [pl.ds(pl.multiple_of((position ^ m) * width, width), width) for m in range(others + 1)]
    hidden = w_up.shape[1]
    slots = gate_in.shape[0]
    half = hidden // 2
    tile = min(512, half)
    through = through_in[...]
    for m in range(others):
        upstream = stacked(parts[m], width, width)
        through = through + folded(w_down.at[:, places[m + 1]], *low_high(upstream))
    through_ref[...] = through.T
    info = stacked(own, full - LANES, LANES).astype(F32)
    lane = lax.broadcasted_iota(jnp.int32, info.shape, 1)
    scale = jnp.sum(jnp.where(lane == expert + E, info, 0.0), axis=1, keepdims=True)
    for m, blocks in enumerate([own] + parts):
        inputs_ref[:, places[m]] = stacked(blocks, 0, width)
        upstream_ref[:, places[m]] = stacked(blocks, width, width)
    xs = [stacked(part, 0, width) for part in parts]
    low = jnp.concatenate([x[:, : width // 2] for x in xs], axis=1)
    high = jnp.concatenate([x[:, width // 2 :] for x in xs], axis=1)
    score = jnp.zeros((slots, 1), F32)
    for start in range(0, hidden, tile):
        units = slice(start, start + tile)
        pre_gate = gate_in[:, units] + dot(low, w_low[:, units], 1, 0) + dot(high, w_high[:, units], 1, 0)
        pre_up = up_in[:, units]
        for m in range(others):
            pre_up = pre_up + dot(xs[m], w_up[places[m + 1], units], 1, 0)
        side, offset = divmod(start, half)
        through = through_ref[side * slots : (side + 1) * slots, offset : offset + tile]
        sig = jax.nn.sigmoid(pre_gate)
        act = pre_gate * sig
        product = act * pre_up
        weighted_ref[:, units] = (scale * product).astype(BF)
        score = score + jnp.sum(through * product, axis=1, keepdims=True)
        scaled = scale * through
        grad_gate_ref[:, units] = (scaled * pre_up * sig * (1.0 + pre_gate * (1.0 - sig))).astype(BF)
        grad_up_ref[:, units] = (scaled * act).astype(BF)
    sub = lax.broadcasted_iota(jnp.int32, (slots, slots), 0)
    diagonal = lax.broadcasted_iota(jnp.int32, (slots, slots), 1)
    spread = jnp.where(sub == diagonal, jnp.broadcast_to(score, (slots, slots)), 0.0)
    routing_ref[...] = jnp.sum(spread, axis=0, keepdims=True)


def halves(row, rows):
    high = row.astype(BF).astype(F32)
    wide = jnp.concatenate([high, row - high], axis=1)
    sub = lax.broadcasted_iota(jnp.int32, (rows, wide.shape[1]), 0)
    return jnp.where(sub == 0, jnp.broadcast_to(wide, sub.shape), 0.0).astype(BF)


def back(position, mask, grad_gate, grad_up, w_low, w_high, w_up, routing_ref, out_ref):
    half = w_low.shape[0]
    width = 2 * half
    low, high = low_high(grad_gate[...])
    rows = pl.ds(pl.multiple_of((position ^ mask) * width, width), width)
    part = dot(w_low[...], low, 1, 1) + dot(w_high[...], high, 1, 1)
    part = part + folded(w_up.at[rows], *low_high(grad_up[...]))
    out_ref[:half, :] = part.astype(out_ref.dtype)
    if out_ref.shape[0] > half:
        out_ref[half:, :] = halves(routing_ref[...], out_ref.shape[0] - half)


def back_other_kernel(others, position_ref, *refs):
    grad_gate, grad_up, w_low, w_high, w_up, routing_ref = refs[:6]
    outs = refs[6:]
    half = w_low.shape[0] // others
    for m, out_ref in enumerate(outs):
        rows = pl.ds(m * half, half)
        weights = w_low.at[rows], w_high.at[rows], w_up
        back(position_ref[0], m + 1, grad_gate, grad_up, *weights, routing_ref, out_ref)


def merge_kernel(order_ref, own_ref, routing_ref, *refs):
    parts, out_ref = refs[:-1], refs[-1]
    half, lanes = own_ref.shape
    slots = lanes // 2
    total = own_ref[...]
    score = routing_ref[...]
    for part in parts:
        total = total + part[:half, :].astype(F32)
        tail = part[half : half + 1, :].astype(F32)
        score = score + tail[:, :slots] + tail[:, slots:]
    columns = jnp.concatenate([total.astype(BF), halves(score, out_ref.shape[1] - half)], axis=0)
    out_ref[...] = dot(order_ref[...], columns, 1, 1).astype(BF)


def plan_kernel(replicas, offsets, position_ref, experts_ref, after_ref, order_ref, *hit_refs):
    size = order_ref.shape[0]
    slots = size // 2
    out_row = lax.broadcasted_iota(jnp.int32, (size, size), 0)
    lane = lax.broadcasted_iota(jnp.int32, (size, size), 1)
    high = lane >= slots
    slot = jnp.where(high, lane - slots, lane)
    block = slot // CAP
    blocks = len(offsets)
    origin = jnp.zeros_like(slot)
    for r in range(replicas):
        for j, offset in enumerate(offsets):
            origin = jnp.where(block == r * blocks + j, offset ^ r, origin)
    origin = origin ^ position_ref[2]
    target = origin * (2 * CAP) + (slot - block * CAP) + jnp.where(high, CAP, 0)
    order_ref[...] = jnp.where(out_row == target, 1.0, 0.0).astype(BF)
    tok = experts_ref.shape[1]
    lane = lax.broadcasted_iota(jnp.int32, (tok, size), 1)
    lane_expert = (lane // (2 * CAP * replicas)).astype(F32)
    hit_first, hit_second, _, before = routing(experts_ref, lane_expert)
    here = before == (lane % CAP).astype(F32)
    low = lane % (2 * CAP) < CAP
    any_hit = (hit_first | hit_second) & here
    for ref, hit in zip(hit_refs, (any_hit & low, any_hit & ~low, hit_first & here, hit_second & here)):
        ref[...] = jnp.where(hit, 1.0, 0.0).astype(BF)


def finish_kernel(back_ref, low_ref, high_ref, first_ref, second_ref, grad_ref, routing_ref):
    tok, width = grad_ref.shape
    half = width // 2
    grad_ref[:, :half] = dot(low_ref[...], back_ref[:, :half], 1, 0).astype(BF)
    grad_ref[:, half:] = dot(high_ref[...], back_ref[:, :half], 1, 0).astype(BF)
    sub = lax.broadcasted_iota(jnp.int32, (tok, tok), 0)
    diagonal = lax.broadcasted_iota(jnp.int32, (tok, tok), 1)
    for k, ref in enumerate((first_ref, second_ref)):
        score = dot(ref[...], back_ref[:, half : half + LANES], 1, 0)[:, :1]
        spread = jnp.where(sub == diagonal, jnp.broadcast_to(score, (tok, tok)), 0.0)
        routing_ref[k : k + 1, :] = jnp.sum(spread, axis=0, keepdims=True)


def outer_kernel(tile, depth, count, *refs):
    lefts, rights, outs = refs[:count], refs[count : 2 * count], refs[2 * count : 3 * count]
    for copy in outer_copies(tile, depth, lefts, rights, outs, *refs[3 * count :]):
        copy.wait()


def outer_back_kernel(tile, depth, position_ref, left, right, grad_up, w_gate, w_up, score_ref, out, kept, *scratch):
    pending = outer_copies(tile, depth, [left], [right], [out], *scratch)
    half = w_gate.shape[0] // 2
    weights = w_gate.at[pl.ds(0, half)], w_gate.at[pl.ds(half, half)], w_up
    back(position_ref[0], 0, right, grad_up, *weights, score_ref, kept)
    for copy in pending:
        copy.wait()


def outer_copies(tile, depth, lefts, rights, outs, buffer, turned, sems):
    steps = []
    for left, right, out in zip(lefts, rights, outs):
        rows, columns = out.shape
        steps += [(left, right, out, start) for start in range(0, rows, tile)]
    copies = []
    for i, (left, right, out, start) in enumerate(steps):
        slot = i % depth
        if start == 0:
            turned[: out.shape[0], :] = left[...].T
        if i >= depth:
            copies[i - depth].wait()
        columns = out.shape[1]
        place = buffer.at[slot, :, pl.ds(0, columns)]
        place[...] = dot(turned[start : start + tile, :], right[...], 1, 0).astype(BF)
        copies.append(pltpu.make_async_copy(place, out.at[pl.ds(start, tile)], sems.at[slot]))
        copies[i].start()
    return copies[max(0, len(copies) - depth) :]


def outer_plan(shapes, slots):
    tile = min([512] + [rows for rows, _ in shapes])
    tile = next(size for size in (tile, 384, 256, 128) if all(rows % size == 0 for rows, _ in shapes))
    depth = 4
    widest = max(columns for _, columns in shapes)
    tallest = max(rows for rows, _ in shapes)
    scratch = [
        pltpu.VMEM((depth, tile, widest), BF),
        pltpu.VMEM((tallest, slots), BF),
        pltpu.SemaphoreType.DMA((depth,)),
    ]
    return tile, depth, scratch


def outer(pairs, name):
    shapes = [(left.shape[1], right.shape[1]) for left, right in pairs]
    slots = pairs[0][0].shape[0]
    tile, depth, scratch = outer_plan(shapes, slots)
    size = sum(rows * columns for rows, columns in shapes)
    return pl.pallas_call(
        functools.partial(outer_kernel, tile, depth, len(pairs)),
        out_shape=[jax.ShapeDtypeStruct(shape, BF) for shape in shapes],
        in_specs=[VMEM] * (2 * len(pairs)),
        out_specs=[ANY] * len(pairs),
        scratch_shapes=scratch,
        compiler_params=params(20),
        cost_estimate=cost(8 * slots * size, 2 * size),
        name=name,
    )(*[left for left, _ in pairs], *[right for _, right in pairs])


def shards(n_wide, n_tensor, tokens, cotangent, gates, experts, w_gate, w_up, w_down):
    axes = ("tensor", "wide")
    replicas = n_wide // E
    wide, tensor = lax.axis_index("wide"), lax.axis_index("tensor")
    tok, width = tokens.shape
    hidden = w_gate.shape[2]
    full = 2 * width + LANES
    slots = n_wide * CAP
    position = jnp.stack([tensor, wide // replicas, wide]).astype(jnp.int32)
    expert = (wide // replicas).astype(jnp.int32)[None]

    def swap(value, wide_mask, tensor_mask):
        pairs = [
            (t * n_wide + w, (t ^ tensor_mask) * n_wide + (w ^ wide_mask))
            for t in range(n_tensor)
            for w in range(n_wide)
        ]
        return lax.ppermute(value, axes, pairs)

    def shape(rows, columns, dtype=BF):
        return jax.ShapeDtypeStruct((rows, columns), dtype)

    experts_t = experts.T
    own = (0,)
    rest = tuple(range(1, n_tensor))
    gathered = pl.pallas_call(
        pack_kernel,
        out_shape=pltpu.VMEM((tok, full), BF),
        in_specs=[ANY] * 4,
        out_specs=VMEM,
        scratch_shapes=[
            pltpu.VMEM((2, tok), BF),
            pltpu.VMEM((2, tok), jnp.int32),
            pltpu.SemaphoreType.DMA((4,)),
        ],
        compiler_params=params(1),
        name="pack",
    )(*[pltpu.with_memory_space_constraint(x, pltpu.HBM) for x in (tokens, cotangent, gates.T, experts_t)])

    gate = w_gate[0]
    up, down = [pltpu.with_memory_space_constraint(w[0], pltpu.VMEM) for w in (w_up, w_down)]
    half = width // 2
    plan = [(own, 0, width), (rest, 0, half), (rest, half, half)]
    staged = []
    offsets = [0]
    mask = n_wide // 2
    while mask >= replicas:
        last = mask == replicas
        got = swap(gathered, mask, 0)
        masks, offset, rows = plan.pop(0)
        kept, token = stage(position, gate, masks, width, offset, rows, gathered)
        staged.append(kept)
        if not last:
            gathered = join(gathered, got, token)
        else:
            early = select(expert, gathered, len(offsets))
            late = select(expert, got, len(offsets), token)
        offsets = offsets + [offset ^ mask for offset in offsets]
        mask //= 2

    wg_own, wg_low, wg_high = staged
    away = [[swap(early, 0, m), swap(late, 0, m)] for m in rest]
    chosen = join(early, late, away[0][0])
    near = [chosen] + [swap(chosen, r, 0) for r in range(1, replicas)]

    others = n_tensor - 1
    partial = pl.pallas_call(
        functools.partial(first_kernel, len(near)),
        out_shape=[shape(slots, hidden, F32)] * 2 + [shape(hidden // 2, 2 * slots, F32)],
        in_specs=[SMEM] + [VMEM] * (len(near) + 3),
        out_specs=[VMEM] * 3,
        compiler_params=params(5),
        cost_estimate=cost(2 * slots * width * hidden, width * hidden // 2),
        name="first",
    )(position, *near, wg_own, up, down)

    order, *hits = pl.pallas_call(
        functools.partial(plan_kernel, replicas, offsets),
        out_shape=[pltpu.VMEM((2 * slots, 2 * slots), BF)] + [pltpu.VMEM((tok, 2 * slots), BF)] * 4,
        in_specs=[SMEM, VMEM, ANY],
        out_specs=[VMEM] * 5,
        compiler_params=params(4),
        name="plan",
    )(position, experts_t, partial[0])
    parts = []
    for early_part, late_part in away:
        part = join(early_part, late_part, partial[0])
        parts.append([part] + [swap(part, r, 0) for r in range(1, replicas)])
    count = len(near)
    weighted, grad_gate, grad_up, inputs, upstream, score = pl.pallas_call(
        functools.partial(second_kernel, count, others),
        out_shape=[shape(slots, hidden)] * 3
        + [shape(slots, width * n_tensor)] * 2
        + [shape(1, slots, F32)],
        in_specs=[SMEM, ANY] + [VMEM] * (count * n_tensor + 7),
        out_specs=[VMEM] * 6,
        scratch_shapes=[pltpu.VMEM((2 * slots, hidden // 2), F32)],
        compiler_params=params(6),
        cost_estimate=cost(24 * slots * width * hidden, 6 * width * hidden),
        name="second",
    )(position, order, *near, *sum(parts, []), wg_low, wg_high, up, down, *partial)

    half = width // 2
    sent = pl.pallas_call(
        functools.partial(back_other_kernel, others),
        out_shape=[shape(half + 16, 2 * slots)] * others,
        in_specs=[SMEM] + [VMEM] * 6,
        out_specs=[VMEM] * others,
        compiler_params=params(5),
        cost_estimate=cost(16 * slots * width * hidden, 4 * width * hidden),
        name="back_other",
    )(position, grad_gate, grad_up, wg_low, wg_high, up, score)
    returned = [swap(value, 0, m) for m, value in zip(rest, sent)]
    grad_shape = (inputs.shape[1], hidden)
    tile, depth, scratch = outer_plan([grad_shape], slots)
    gate_proj_grad, kept = pl.pallas_call(
        functools.partial(outer_back_kernel, tile, depth),
        out_shape=[jax.ShapeDtypeStruct(grad_shape, BF), shape(half, 2 * slots, F32)],
        in_specs=[SMEM] + [VMEM] * 6,
        out_specs=[ANY, VMEM],
        scratch_shapes=scratch,
        compiler_params=params(16),
        cost_estimate=cost(8 * slots * grad_shape[0] * hidden, 2 * grad_shape[0] * hidden),
        name="gate_grad",
    )(position, inputs, grad_gate, grad_up, wg_own, up, score)
    merged = pl.pallas_call(
        merge_kernel,
        out_shape=shape(2 * slots, half + LANES),
        in_specs=[VMEM] * (3 + others),
        out_specs=VMEM,
        compiler_params=params(4),
        name="merge",
    )(order, kept, score, *returned)
    landed = lax.all_to_all(merged, "wide", split_axis=0, concat_axis=0, tiled=True)
    up_proj_grad, down_proj_grad = outer([(inputs, grad_up), (weighted, upstream)], "other_grads")
    input_grad, routing_grad = pl.pallas_call(
        finish_kernel,
        out_shape=[shape(tok, width), shape(2, tok, F32)],
        in_specs=[VMEM] * 5,
        out_specs=[VMEM] * 2,
        compiler_params=params(3),
        name="finish",
    )(landed, *hits)
    return (
        input_grad,
        routing_grad.T,
        gate_proj_grad[None],
        up_proj_grad[None],
        down_proj_grad[None],
    )


def solution(mesh):
    return jax.shard_map(
        functools.partial(shards, mesh.shape["wide"], mesh.shape["tensor"]),
        mesh=mesh,
        in_specs=(
            P("wide", "tensor"),
            P("wide", "tensor"),
            P("wide", None),
            P("wide", None),
            P("wide", None, "tensor"),
            P("wide", None, "tensor"),
            P("wide", "tensor", None),
        ),
        out_specs=(
            P("wide", "tensor"),
            P("wide", None),
            P("wide", None, "tensor"),
            P("wide", None, "tensor"),
            P("wide", "tensor", None),
        ),
        check_vma=False,
    )
```
